128 devices in a mesh: section: 8 (over z, y_lo), shard: 16 (over y_hi, x, core).
Axes of the slice: x: 4, y: 4 (y_hi: 2, y_lo: 2; y = y_hi * 2 + y_lo), z: 4, core: 2. Of those that a mesh axis runs over, the one named last changes fastest.
Arguments:
- saved_inputs: bfloat16 [8, 8192, 2048], P('section', 'shard'), may hold values from -6 to 6
- grad_out: bfloat16 [8192, 2048], P('shard'), may hold values from -6 to 6
- w_in: bfloat16 [8, 2048, 4096], P('section', 'shard'), may hold values from -0.125 to 0.125
- w_out: bfloat16 [8, 4096, 2048], P('section', 'shard'), may hold values from -0.09375 to 0.09375
- skip_gain: float32 [4, 2048], replicated, may hold values from 0.5 to 1.5
- proj_model: bfloat16 [8, 2048, 128], P('section'), may hold values from -0.125 to 0.125
- proj_hidden: bfloat16 [8, 4096, 128], P('section'), may hold values from -0.09375 to 0.09375
Outputs:
- features: float32 [32, 4096], P('shard', 'section')
The draws below stay inside these ranges and needn't reach their ends.
All inputs are finite; a program needn't handle non-finite values.
Results may differ from the reference program's by a relative error of at most 0.02.
Values may be sent and summed in bfloat16 or wider, within the bound.
A program may use at most 128 MiB of HBM per device.

```python
import math
import jax
import jax.numpy as jnp
from jax import lax

D = 2048
FF = 4096
PROJ = 64
SEQ = 256
SAMPLES = 32
TOKENS = 8192
SECTION_COUNT = 8


def levels(key, dims, shards, smallest, top_value):
    gain, own = 1.0, jax.random.fold_in(key, 6)
    for dim, parts in shards:
        heights = jnp.exp(jax.random.uniform(jax.random.fold_in(own, dim), (parts,), jnp.float32, smallest / len(shards), top_value / len(shards)))
        gain = gain * jnp.repeat(heights, dims[dim] // parts).reshape([-1 if axis == dim else 1 for axis in range(len(dims))])
    return gain


def normal_values(key, shape, width, most, pieces=(), dtype=jnp.bfloat16):
    array = width * jax.random.normal(key, shape, jnp.float32)
    if pieces:
        array = array * levels(key, shape, pieces, -0.22, 0.18)
    return jnp.clip(array, -most, most).astype(dtype)


def setup_inputs(seed: int = 0) -> dict:
    keys = jax.random.split(jax.random.key(seed), 8)
    return {
        "saved_inputs": normal_values(keys[0], (SECTION_COUNT, TOKENS, D), 1.0, 6.0, ((0, 8), (1, 16))),
        "grad_out": normal_values(keys[1], (TOKENS, D), 1.0, 6.0, ((0, 16),)),
        "w_in": normal_values(keys[2], (SECTION_COUNT, D, FF), D ** -0.5, 0.125, ((0, 8), (1, 16))),
        "w_out": normal_values(keys[3], (SECTION_COUNT, FF, D), FF ** -0.5, 0.09375, ((0, 8), (1, 16))),
        "skip_gain": jnp.clip(jax.random.uniform(keys[4], (SECTION_COUNT // 2, D), jnp.float32, 0.5, 1.5), 0.5, 1.5),
        "proj_model": normal_values(keys[5], (SECTION_COUNT, D, 2 * PROJ), D ** -0.5, 0.125, ((0, 8),)),
        "proj_hidden": normal_values(keys[6], (SECTION_COUNT, FF, 2 * PROJ), FF ** -0.5, 0.09375, ((0, 8),)),
    }


square_root_half = 1.0 / math.sqrt(2.0)
inv_root_two_pi = 1.0 / math.sqrt(2.0 * math.pi)

def matmul(left_operand, right_operand):
    return jnp.dot(left_operand.astype(jnp.float32), right_operand.astype(jnp.float32), precision=lax.Precision.HIGHEST)

def gelu_parts(value):
    cumulative = 0.5 * (1.0 + jax.scipy.special.erf(value * square_root_half))
    density = jnp.exp(-0.5 * value * value) * inv_root_two_pi
    return (value * cumulative, cumulative + value * density)

def per_sample(left_operand, right_operand):
    left_operand = left_operand.reshape(SAMPLES, SEQ, PROJ)
    right_operand = right_operand.reshape(SAMPLES, SEQ, PROJ)
    return jnp.einsum('anf,anj->afj', left_operand, right_operand, precision=lax.Precision.HIGHEST)

def reference(saved_inputs, grad_out, w_in, w_out, skip_gain, proj_model, proj_hidden):
    half = SECTION_COUNT // 2
    carried = grad_out
    skips = {}
    total = jnp.zeros((SAMPLES, PROJ, PROJ), jnp.float32)
    for section in range(SECTION_COUNT - 1, -1, -1):
        if section < half:
            grad = (carried.astype(jnp.float32) + skips[section].astype(jnp.float32)).astype(jnp.bfloat16)
        else:
            grad = carried
        inputs = saved_inputs[section]
        pre_act = matmul(inputs, w_in[section])
        act, slope = gelu_parts(pre_act)
        hidden = act.astype(jnp.bfloat16)
        grad_hidden = matmul(grad, w_out[section].T)
        grad_pre = (grad_hidden * slope).astype(jnp.bfloat16)
        grad_x = grad.astype(jnp.float32) + matmul(grad_pre, w_in[section].T)
        carried = grad_x.astype(jnp.bfloat16)
        if section >= half:
            skips[SECTION_COUNT - 1 - section] = (grad_x * skip_gain[section - half][None, :]).astype(jnp.bfloat16)
        in_first = matmul(inputs, proj_model[section][:, :PROJ])
        out_first = matmul(grad_pre, proj_hidden[section][:, :PROJ])
        in_second = matmul(hidden, proj_hidden[section][:, PROJ:])
        out_second = matmul(grad, proj_model[section][:, PROJ:])
        total = total + per_sample(in_first, out_first) + per_sample(in_second, out_second)
    return (total * SEQ ** (-0.5)).reshape(SAMPLES, PROJ * PROJ)
```

```python
import functools
import math

import jax
import jax.numpy as jnp
from jax import lax
from jax.experimental import pallas as pl
from jax.experimental.pallas import tpu as pltpu
from jax.sharding import PartitionSpec as P

MESH = pl.DeviceIdType.MESH
SEQ = 256
SECTIONS = 8
CHIPS = 8
PIECES = 4
CHUNKS = 4
square_root_half = 1.0 / math.sqrt(2.0)
inv_root_two_pi = 1.0 / math.sqrt(2.0 * math.pi)

POSITIONS = ("own", "xm", "xp", "x2a", "x2b", "yo", "pm", "pp", "p2a", "p2b")
ITEMS = (
    ("in", 0, 1792, False),
    ("in", 1792, 2304, True),
    ("out", 0, 896, False),
    ("out", 896, 1152, True),
)
EVENTS = {}
for _item in range(len(ITEMS)):
    for _pos in POSITIONS:
        if _pos != "own":
            EVENTS[(_item, _pos, "link")] = len(EVENTS)
        EVENTS[(_item, _pos, "core")] = len(EVENTS)


def forwards(pos, y_first):
    table = {
        "own": [("xm", "right"), ("xp", "left"), ("yo", "across")],
        "xm": [("x2a", "right")],
        "xp": [("x2b", "left")],
        "x2a": [],
        "x2b": [],
        "yo": [],
        "pm": [],
        "pp": [],
        "p2a": [],
        "p2b": [],
    }
    if y_first:
        table["yo"] = [("pm", "right"), ("pp", "left")]
        table["pm"] = [("p2a", "right")]
        table["pp"] = [("p2b", "left")]
    else:
        table["xm"] = table["xm"] + [("pm", "across")]
        table["xp"] = table["xp"] + [("pp", "across")]
        table["x2a"] = [("p2a", "across")]
        table["x2b"] = [("p2b", "across")]
    return table[pos]


def gelu_parts(value):
    cumulative = 0.5 * (1.0 + lax.erf(value * square_root_half))
    density = jnp.exp(-0.5 * value * value) * inv_root_two_pi
    return (value * cumulative, cumulative + value * density)


def nt(a, b):
    return lax.dot_general(a, b, (((1,), (1,)), ((), ())), preferred_element_type=jnp.float32)


def nn(a, b):
    return jnp.dot(a, b, preferred_element_type=jnp.float32)


def kernel(
    x_ref, g_ref, wi_ref, wo_ref, gain_ref, pm_ref, ph_ref, out_ref,
    wi, wo, xs, slope, inbox, skipbox, stage, gu, acc, in_a, in_b, term, parts,
    load_sem, ssem, rsem, swap_ssem, swap_rsem,
    next_ssem, next_rsem, skip_ssem, skip_rsem, last_ssem, last_rsem,
):
    s = lax.axis_index("section")
    h = lax.axis_index("shard")
    yh, x, c = h // 8, (h // 2) % 4, h % 2
    even = lax.rem(s, 2) == 0
    tokens, width = xs.shape
    hidden_width = slope.shape[1]
    piece = tokens // PIECES
    chunk = width // CHUNKS
    tile = 256

    def device(section, hi, xx, core):
        return (section, hi * 8 + xx * 2 + core)

    right = device(s, yh, (x + 1) % 4, c)
    left = device(s, yh, (x + 3) % 4, c)
    across = device(s, 1 - yh, x, c)
    sibling = device(s, yh, x, 1 - c)
    crossed = (yh + c) % 2
    below = device(jnp.maximum(s - 1, 0), crossed, x, c)
    mirror = device(SECTIONS - 1 - s, crossed, x, c)
    home_hi = jnp.where(even, crossed, yh)
    toward = {"right": right, "left": left, "across": across}

    barrier = pltpu.get_barrier_semaphore()
    for there in (right, left, sibling, across):
        pl.semaphore_signal(barrier, inc=1, device_id=there, device_id_type=MESH)
    for step in range(1, SECTIONS):
        for hi in range(2):
            pl.semaphore_signal(
                barrier, inc=1, device_id=device((s + step) % SECTIONS, hi, x, c), device_id_type=MESH
            )

    own_chip = yh * 4 + x
    load_in = pltpu.make_async_copy(
        wi_ref, wi.at[own_chip, :, pl.ds(pl.multiple_of(c * 128, 128), 128)], load_sem.at[0]
    )
    load_out = pltpu.make_async_copy(wo_ref, wo.at[h], load_sem.at[1])
    load_x = pltpu.make_async_copy(x_ref, xs, load_sem.at[2])
    load_g = pltpu.make_async_copy(g_ref, inbox, load_sem.at[3])
    load_in.start()
    load_out.start()
    swapped = even & (c == 1)

    @pl.when(jnp.logical_not(swapped))
    def _():
        load_x.start()

    @pl.when(s == SECTIONS - 1)
    def _():
        load_g.start()

    load_in.wait()
    load_out.wait()

    @pl.when(jnp.logical_not(swapped))
    def _():
        load_x.wait()

    @pl.when(s == SECTIONS - 1)
    def _():
        load_g.wait()

    pl.semaphore_wait(barrier, 4 + 2 * (SECTIONS - 1))

    def slab(item, pos, core):
        array, first, rows, _ = ITEMS[item]
        hi = yh if pos in ("own", "xm", "xp", "x2a", "x2b") else 1 - yh
        step = {"own": 0, "yo": 0, "xm": 3, "pm": 3, "xp": 1, "pp": 1}.get(pos, 2)
        half = pos[-1] if pos[-1] in "ab" else ""
        return slab_at(array, hi * 4 + (x + step) % 4, core, first, rows, half)

    def slab_at(array, chip, core, first, rows, half):
        if half:
            rows = rows // 2
            first = first + (rows if half == "b" else 0)
        if array == "in":
            return wi.at[chip, pl.ds(first, rows), pl.ds(pl.multiple_of(core * 128, 128), 128)]
        return wo.at[chip * 2 + core, pl.ds(first, rows), :]

    def copy_of(item, pos, kind, src, there):
        event = EVENTS[(item, pos, kind)]
        return pltpu.make_async_remote_copy(
            src_ref=src, dst_ref=src, send_sem=ssem.at[event], recv_sem=rsem.at[event],
            device_id=there, device_id_type=MESH,
        )

    def source(item, pos, there_pos):
        array, first, rows, _ = ITEMS[item]
        half = there_pos[-1] if there_pos[-1] in "ab" else ""
        hi = yh if pos in ("own", "xm", "xp", "x2a", "x2b") else 1 - yh
        step = {"own": 0, "yo": 0, "xm": 3, "pm": 3, "xp": 1, "pp": 1}.get(pos, 2)
        return slab_at(array, hi * 4 + (x + step) % 4, c, first, rows, half)

    sends = []

    def pass_on(item, pos):
        for there_pos, direction in forwards(pos, ITEMS[item][3]):
            cp = copy_of(item, there_pos, "link", source(item, pos, there_pos), toward[direction])
            cp.start()
            sends.append((item, pos, there_pos, direction))
        cp = copy_of(item, pos, "core", slab(item, pos, c), sibling)
        cp.start()
        sends.append((item, pos, pos, "core"))

    def receive(item, pos):
        copy_of(item, pos, "link", slab(item, pos, c), sibling).wait_recv()
        pass_on(item, pos)

    def receive_core(item, pos):
        copy_of(item, pos, "core", slab(item, pos, 1 - c), sibling).wait_recv()

    pass_on(0, "own")
    pass_on(1, "own")
    swap_x = pltpu.make_async_remote_copy(
        src_ref=x_ref, dst_ref=xs, send_sem=swap_ssem, recv_sem=swap_rsem, device_id=across, device_id_type=MESH
    )

    @pl.when(swapped)
    def _():
        swap_x.start()

    for item, pos in (
        (0, "xm"), (0, "xp"), (1, "yo"), (1, "xm"), (1, "xp"), (0, "yo"), (0, "x2a"), (0, "x2b"),
    ):
        receive(item, pos)
    pass_on(2, "own")
    pass_on(3, "own")
    for item, pos in (
        (1, "pm"), (1, "pp"), (0, "pm"), (0, "pp"), (1, "x2a"), (1, "x2b"),
        (2, "xm"), (2, "xp"),
        (0, "p2a"), (0, "p2b"), (1, "p2a"), (1, "p2b"),
    ):
        receive(item, pos)
    for item in (0, 1):
        for pos in POSITIONS:
            receive_core(item, pos)

    @pl.when(swapped)
    def _():
        swap_x.wait_recv()

    in_a[...] = nn(xs[...], pm_ref[...])
    in_b[...] = jnp.zeros_like(in_b)
    late = (
        (3, "yo"), (3, "xm"), (3, "xp"), (2, "yo"), (2, "x2a"), (2, "x2b"), (3, "pm"), (3, "pp"),
        (2, "pm"), (2, "pp"), (3, "x2a"), (3, "x2b"), (2, "p2a"), (2, "p2b"), (3, "p2a"), (3, "p2b"),
    )
    steps = hidden_width // tile

    @pl.loop(0, steps)
    def _(i):
        for at, (item, pos) in enumerate(late):
            @pl.when(i == at * steps // len(late))
            def _():
                receive(item, pos)

        cols = pl.ds(pl.multiple_of(i * tile, tile), tile)
        for part in range(tokens // 256):
            rows = pl.ds(part * 256, 256)
            u = nt(xs[rows, 0:tile], wi[0, cols, :])
            for chip in range(1, CHIPS):
                u = u + nt(xs[rows, chip * tile:(chip + 1) * tile], wi[chip, cols, :])
            act, slant = gelu_parts(u)
            slope[rows, cols] = slant
            in_b[rows, :] += nn(act.astype(jnp.bfloat16), ph_ref[cols, :])

    for item in (2, 3):
        for pos in POSITIONS:
            receive_core(item, pos)

    def chunk_copy(p, d, src, dst, send, recv, there):
        where = (pl.ds(pl.multiple_of(p * piece, piece), piece), pl.ds(d * chunk, chunk))
        return pltpu.make_async_remote_copy(
            src_ref=src.at[where], dst_ref=dst.at[where], send_sem=send.at[p, d], recv_sem=recv.at[p, d],
            device_id=there, device_id_type=MESH,
        )

    def to_next(p, d):
        return chunk_copy(p, d, stage, inbox, next_ssem, next_rsem, below)

    def to_skip(p, d):
        return chunk_copy(p, d, stage, skipbox, skip_ssem, skip_rsem, mirror)

    half = SECTIONS // 2
    gain_row = jnp.clip(half - 1 - s, 0, half - 1)

    @pl.loop(0, PIECES)
    def _(p):
        rows = pl.ds(pl.multiple_of(p * piece, piece), piece)
        for part in range(2):
            cols = pl.ds(part * (width // 2), width // 2)

            @pl.when(s < SECTIONS - 1)
            def _():
                for d in range(part * CHUNKS // 2, (part + 1) * CHUNKS // 2):
                    to_next(p, d).wait_recv()

            @pl.when(s < half - 1)
            def _():
                for d in range(part * CHUNKS // 2, (part + 1) * CHUNKS // 2):
                    to_skip(p, d).wait_recv()
                gain = gain_ref[pl.ds(gain_row, 1), cols]
                total = inbox[rows, cols].astype(jnp.float32) + gain * skipbox[rows, cols].astype(jnp.float32)
                inbox[rows, cols] = total.astype(jnp.bfloat16)

            @pl.when(s == half - 1)
            def _():
                gain = gain_ref[pl.ds(gain_row, 1), cols]
                value = inbox[rows, cols].astype(jnp.float32)
                inbox[rows, cols] = (value + gain * value).astype(jnp.bfloat16)

            @pl.loop(0, hidden_width // tile)
            def _(j):
                there = pl.ds(pl.multiple_of(j * tile, tile), tile)
                product = nn(inbox[rows, cols], wo[j, cols, :])
                if part == 0:
                    acc[:, there] = product
                else:
                    gu[rows, there] = ((acc[:, there] + product) * slope[rows, there]).astype(jnp.bfloat16)

        @pl.when(s > 0)
        def _():
            for d in range(CHUNKS):
                @pl.loop(0, chunk // tile)
                def _(k):
                    there = pl.ds(pl.multiple_of(d * chunk + k * tile, tile), tile)
                    grad_x = nn(gu[rows, :], wi[d * (chunk // tile) + k])
                    stage[rows, there] = (inbox[rows, there].astype(jnp.float32) + grad_x).astype(jnp.bfloat16)

                to_next(p, d).start()

                @pl.when(s > half)
                def _():
                    to_skip(p, d).start()

    for sample in range(tokens // SEQ):
        rows = pl.ds(sample * SEQ, SEQ)
        out_a = nn(gu[rows, :], ph_ref[...])
        out_b = nn(inbox[rows, :], pm_ref[...])

        def outer(a, b):
            return lax.dot_general(
                a, b, (((0,), (0,)), ((), ())), precision=lax.Precision.HIGHEST,
                preferred_element_type=jnp.float32,
            )

        first = outer(in_a[rows, :], out_a)
        second = pltpu.roll(outer(in_b[rows, :], out_b), 64, 1)
        term[sample] = (first[0:64, :] + second[64:128, :]) * (SEQ ** -0.5)

    def last_copy(t, index):
        return pltpu.make_async_remote_copy(
            src_ref=term.at[:, pl.ds(t * 8, 8), :], dst_ref=parts.at[index], send_sem=last_ssem.at[t],
            recv_sem=last_rsem.at[index], device_id=device(t, home_hi, x, c), device_id_type=MESH,
        )

    for t in range(SECTIONS):
        stays = (s == t) & jnp.logical_not(swapped)

        @pl.when(stays)
        def _():
            parts[t] = term[:, t * 8:(t + 1) * 8, :]

        @pl.when(jnp.logical_not(stays))
        def _():
            last_copy(t, s).start()

    for item, pos, there_pos, direction in sends:
        if direction == "core":
            copy_of(item, pos, "core", slab(item, pos, c), sibling).wait_send()
        else:
            copy_of(item, there_pos, "link", source(item, pos, there_pos), toward[direction]).wait_send()

    @pl.when(swapped)
    def _():
        swap_x.wait_send()

    @pl.loop(0, PIECES)
    def _(p):
        for d in range(CHUNKS):
            @pl.when(s > 0)
            def _():
                to_next(p, d).wait_send()

            @pl.when(s > half)
            def _():
                to_skip(p, d).wait_send()

    for t in range(SECTIONS):
        stays = (s == t) & jnp.logical_not(swapped)

        @pl.when(jnp.logical_not(stays))
        def _():
            last_copy(t, s).wait_send()
            last_copy(t, t).wait_recv()

    total = parts[0]
    for t in range(1, SECTIONS):
        total = total + parts[t]
    out_ref[...] = total


def body(saved_inputs, grad_out, w_in, w_out, skip_gain, proj_model, proj_hidden):
    tokens, width = grad_out.shape
    hidden_width = w_in.shape[2]
    samples = tokens // SEQ
    bf16, f32 = jnp.bfloat16, jnp.float32
    dma = pltpu.SemaphoreType.DMA
    result = pl.pallas_call(
        kernel,
        out_shape=jax.ShapeDtypeStruct((samples, 8, 128), f32),
        in_specs=[pl.BlockSpec(memory_space=pl.ANY)] * 4 + [pl.BlockSpec(memory_space=pltpu.VMEM)] * 3,
        out_specs=pl.BlockSpec(memory_space=pltpu.VMEM),
        scratch_shapes=[
            pltpu.VMEM((CHIPS, hidden_width, 256), bf16),
            pltpu.VMEM((2 * CHIPS, width, 256), bf16),
            pltpu.VMEM((tokens, width), bf16),
            pltpu.VMEM((tokens, hidden_width), f32),
            pltpu.VMEM((tokens, width), bf16),
            pltpu.VMEM((tokens, width), bf16),
            pltpu.VMEM((tokens, width), bf16),
            pltpu.VMEM((tokens, hidden_width), bf16),
            pltpu.VMEM((tokens // PIECES, hidden_width), f32),
            pltpu.VMEM((tokens, 128), f32),
            pltpu.VMEM((tokens, 128), f32),
            pltpu.VMEM((samples, 64, 128), f32),
            pltpu.VMEM((SECTIONS, samples, 8, 128), f32),
            dma((4,)),
            dma((len(EVENTS),)),
            dma((len(EVENTS),)),
            dma,
            dma,
            dma((PIECES, CHUNKS)),
            dma((PIECES, CHUNKS)),
            dma((PIECES, CHUNKS)),
            dma((PIECES, CHUNKS)),
            dma((SECTIONS,)),
            dma((SECTIONS,)),
        ],
        compiler_params=pltpu.CompilerParams(
            collective_id=0, has_side_effects=True, vmem_limit_bytes=62 * 2**20
        ),
    )(saved_inputs[0], grad_out, w_in[0].T, w_out[0].T, skip_gain, proj_model[0], proj_hidden[0])
    return result[:, :, :64].reshape(samples, 512)


def solution(mesh):
    placed = (
        P("section", "shard", None),
        P("shard", None),
        P("section", "shard", None),
        P("section", "shard", None),
        P(),
        P("section", None, None),
        P("section", None, None),
    )
    return jax.shard_map(
        body, mesh=mesh, in_specs=placed, out_specs=P("shard", "section"), check_vma=False
    )
```

```python
import functools
import math

import jax
import jax.numpy as jnp
from jax import lax
from jax.experimental import pallas as pl
from jax.experimental.pallas import tpu as pltpu
from jax.sharding import PartitionSpec as P

MESH = pl.DeviceIdType.MESH
SEQ = 256
SECTIONS = 8
CHIPS = 8
PIECES = 4
CHUNKS = 4
PARTS = 2
square_root_half = 1.0 / math.sqrt(2.0)
inv_root_two_pi = 1.0 / math.sqrt(2.0 * math.pi)

POSITIONS = ("own", "xm", "xp", "x2a", "x2b", "yo", "pm", "pp", "p2a", "p2b")
ITEMS = (
    ("in", 0, 1792, False),
    ("in", 1792, 2304, True),
    ("out", 0, 896, False),
    ("out", 896, 1152, True),
)
EVENTS = {}
for _item in range(len(ITEMS)):
    for _pos in POSITIONS:
        if _pos != "own":
            EVENTS[(_item, _pos, "link")] = len(EVENTS)
        EVENTS[(_item, _pos, "core")] = len(EVENTS)


EARLY = (
    (0, "own"), (1, "own"),
    (0, "xm"), (0, "xp"), (1, "yo"), (1, "xm"), (1, "xp"), (0, "yo"), (0, "x2a"), (0, "x2b"),
    (2, "own"), (3, "own"), "swap",
    (1, "pm"), (1, "pp"), (0, "pm"), (0, "pp"), (1, "x2a"), (1, "x2b"), (2, "xm"), (2, "xp"),
    (0, "p2a"), (0, "p2b"), (1, "p2a"), (1, "p2b"),
)
LATE = (
    (3, "yo"), (3, "xm"), (3, "xp"), (2, "yo"), (2, "x2a"), (2, "x2b"), (3, "pm"), (3, "pp"),
    (2, "pm"), (2, "pp"), (3, "x2a"), (3, "x2b"), (2, "p2a"), (2, "p2b"), (3, "p2a"), (3, "p2b"),
)


def forwards(pos, y_first):
    table = {
        "own": [("xm", "right"), ("xp", "left"), ("yo", "across")],
        "xm": [("x2a", "right")],
        "xp": [("x2b", "left")],
        "x2a": [],
        "x2b": [],
        "yo": [],
        "pm": [],
        "pp": [],
        "p2a": [],
        "p2b": [],
    }
    if y_first:
        table["yo"] = [("pm", "right"), ("pp", "left")]
        table["pm"] = [("p2a", "right")]
        table["pp"] = [("p2b", "left")]
    else:
        table["xm"] = table["xm"] + [("pm", "across")]
        table["xp"] = table["xp"] + [("pp", "across")]
        table["x2a"] = [("p2a", "across")]
        table["x2b"] = [("p2b", "across")]
    return table[pos]


def gelu_parts(value):
    cumulative = 0.5 * (1.0 + lax.erf(value * square_root_half))
    density = jnp.exp(-0.5 * value * value) * inv_root_two_pi
    return (value * cumulative, cumulative + value * density)


def nt(a, b):
    return lax.dot_general(a, b, (((1,), (1,)), ((), ())), preferred_element_type=jnp.float32)


def nn(a, b):
    return jnp.dot(a, b, preferred_element_type=jnp.float32)


def kernel(
    x_ref, g_ref, wi_ref, wo_ref, gain_ref, pm_ref, ph_ref, out_ref,
    wi, wo, xs, slope, inbox, skipbox, stage, gu, acc, in_a, in_b, term, parts,
    load_sem, ssem, rsem, swap_ssem, swap_rsem,
    next_ssem, next_rsem, skip_ssem, skip_rsem, last_ssem, last_rsem, turn_sem,
):
    s = lax.axis_index("section")
    h = lax.axis_index("shard")
    yh, x, c = h // 8, (h // 2) % 4, h % 2

    def crosses(section):
        return (lax.rem(section, 2) == 0) & (section < SECTIONS - 2)

    tokens, width = xs.shape
    hidden_width = slope.shape[1]
    piece = tokens // PIECES
    chunk = width // CHUNKS
    tile = 256

    def device(section, hi, xx, core):
        return (section, hi * 8 + xx * 2 + core)

    right = device(s, yh, (x + 1) % 4, c)
    left = device(s, yh, (x + 3) % 4, c)
    across = device(s, 1 - yh, x, c)
    sibling = device(s, yh, x, 1 - c)
    swapped = crosses(s) & (c == 1)

    def facing(section):
        cross = (crosses(s) | crosses(section)) & (c == 1)
        return device(section, jnp.where(cross, 1 - yh, yh), x, c)

    below = facing(jnp.maximum(s - 1, 0))
    mirror = facing(SECTIONS - 1 - s)
    home_hi = jnp.where(swapped, 1 - yh, yh)
    toward = {"right": right, "left": left, "across": across}

    barrier = pltpu.get_barrier_semaphore()
    for there in (right, left, sibling, across):
        pl.semaphore_signal(barrier, inc=1, device_id=there, device_id_type=MESH)
    for step in range(1, SECTIONS):
        for hi in range(2):
            pl.semaphore_signal(
                barrier, inc=1, device_id=device((s + step) % SECTIONS, hi, x, c), device_id_type=MESH
            )

    own_chip = yh * 4 + x
    slab_in, slab_out = wi_ref.shape[1], wo_ref.shape[1]
    load_in = pltpu.make_async_copy(wi_ref.at[0], gu.at[pl.ds(0, slab_in)], load_sem.at[0])
    load_out = pltpu.make_async_copy(wo_ref.at[0], stage.at[pl.ds(0, slab_out)], load_sem.at[1])
    load_x = pltpu.make_async_copy(x_ref.at[0], xs, load_sem.at[2])
    load_g = pltpu.make_async_copy(g_ref, inbox, load_sem.at[3])
    load_in.start()
    load_out.start()
    @pl.when(jnp.logical_not(swapped))
    def _():
        load_x.start()

    @pl.when(s == SECTIONS - 1)
    def _():
        load_g.start()

    load_in.wait()
    own_cols = pl.ds(pl.multiple_of(c * slab_in, slab_in), slab_in)
    for first in range(0, hidden_width, 512):
        wi[own_chip, first:first + 512, own_cols] = gu[0:slab_in, first:first + 512].T
    load_out.wait()
    for first in range(0, width, 512):
        wo[h, first:first + 512, :] = stage[0:slab_out, first:first + 512].T

    @pl.when(jnp.logical_not(swapped))
    def _():
        load_x.wait()

    @pl.when(s == SECTIONS - 1)
    def _():
        load_g.wait()

    pl.semaphore_wait(barrier, 4 + 2 * (SECTIONS - 1))

    def slab(item, pos, core):
        array, first, rows, _ = ITEMS[item]
        hi = yh if pos in ("own", "xm", "xp", "x2a", "x2b") else 1 - yh
        step = {"own": 0, "yo": 0, "xm": 3, "pm": 3, "xp": 1, "pp": 1}.get(pos, 2)
        half = pos[-1] if pos[-1] in "ab" else ""
        return slab_at(array, hi * 4 + (x + step) % 4, core, first, rows, half)

    def slab_at(array, chip, core, first, rows, half):
        if half:
            rows = rows // 2
            first = first + (rows if half == "b" else 0)
        if array == "in":
            return wi.at[chip, pl.ds(first, rows), pl.ds(pl.multiple_of(core * 128, 128), 128)]
        return wo.at[chip * 2 + core, pl.ds(first, rows), :]

    def copy_of(item, pos, kind, src, there):
        event = EVENTS[(item, pos, kind)]
        return pltpu.make_async_remote_copy(
            src_ref=src, dst_ref=src, send_sem=ssem.at[event], recv_sem=rsem.at[event],
            device_id=there, device_id_type=MESH,
        )

    def source(item, pos, there_pos):
        array, first, rows, _ = ITEMS[item]
        half = there_pos[-1] if there_pos[-1] in "ab" else ""
        hi = yh if pos in ("own", "xm", "xp", "x2a", "x2b") else 1 - yh
        step = {"own": 0, "yo": 0, "xm": 3, "pm": 3, "xp": 1, "pp": 1}.get(pos, 2)
        return slab_at(array, hi * 4 + (x + step) % 4, c, first, rows, half)

    sends = []

    def pass_on(item, pos):
        for there_pos, direction in forwards(pos, ITEMS[item][3]):
            cp = copy_of(item, there_pos, "link", source(item, pos, there_pos), toward[direction])
            cp.start()
            sends.append((item, pos, there_pos, direction))
        cp = copy_of(item, pos, "core", slab(item, pos, c), sibling)
        cp.start()
        sends.append((item, pos, pos, "core"))

    def receive(item, pos):
        copy_of(item, pos, "link", slab(item, pos, c), sibling).wait_recv()
        pass_on(item, pos)

    def receive_core(item, pos):
        copy_of(item, pos, "core", slab(item, pos, 1 - c), sibling).wait_recv()

    swap_x = pltpu.make_async_remote_copy(
        src_ref=x_ref.at[0], dst_ref=xs, send_sem=swap_ssem, recv_sem=swap_rsem, device_id=across, device_id_type=MESH
    )
    for entry in EARLY:
        if entry == "swap":
            @pl.when(swapped)
            def _():
                swap_x.start()
        elif entry[1] == "own":
            pass_on(*entry)
        else:
            receive(*entry)
    for item in (0, 1):
        for pos in POSITIONS:
            receive_core(item, pos)

    @pl.when(swapped)
    def _():
        swap_x.wait_recv()

    in_a[...] = nn(xs[...], pm_ref[...])
    in_b[...] = jnp.zeros_like(in_b)
    steps = hidden_width // tile

    @pl.loop(0, steps)
    def _(i):
        for at, (item, pos) in enumerate(LATE):
            @pl.when(i == at * steps // len(LATE))
            def _():
                receive(item, pos)

        cols = pl.ds(pl.multiple_of(i * tile, tile), tile)
        for part in range(tokens // 256):
            rows = pl.ds(part * 256, 256)
            u = nt(xs[rows, 0:tile], wi[0, cols, :])
            for chip in range(1, CHIPS):
                u = u + nt(xs[rows, chip * tile:(chip + 1) * tile], wi[chip, cols, :])
            act, slant = gelu_parts(u)
            slope[rows, cols] = slant
            in_b[rows, :] += nn(act.astype(jnp.bfloat16), ph_ref[cols, :])

    for item in (2, 3):
        for pos in POSITIONS:
            receive_core(item, pos)

    def chunk_copy(p, d, src, dst, send, recv, there):
        where = (pl.ds(pl.multiple_of(p * piece, piece), piece), pl.ds(d * chunk, chunk))
        return pltpu.make_async_remote_copy(
            src_ref=src.at[where], dst_ref=dst.at[where], send_sem=send.at[p, d], recv_sem=recv.at[p, d],
            device_id=there, device_id_type=MESH,
        )

    def to_next(p, d):
        return chunk_copy(p, d, stage, inbox, next_ssem, next_rsem, below)

    def to_skip(p, d):
        return chunk_copy(p, d, stage, skipbox, skip_ssem, skip_rsem, mirror)

    half = SECTIONS // 2
    gain_row = jnp.clip(half - 1 - s, 0, half - 1)

    @pl.loop(0, PIECES)
    def _(p):
        rows = pl.ds(pl.multiple_of(p * piece, piece), piece)
        for part in range(PARTS):
            cols = pl.ds(part * (width // PARTS), width // PARTS)
            chunks = range(part * CHUNKS // PARTS, (part + 1) * CHUNKS // PARTS)

            @pl.when(s < SECTIONS - 1)
            def _():
                for d in chunks:
                    to_next(p, d).wait_recv()

            @pl.when(s < half - 1)
            def _():
                for d in chunks:
                    to_skip(p, d).wait_recv()
                gain = gain_ref[pl.ds(gain_row, 1), cols]
                total = inbox[rows, cols].astype(jnp.float32) + gain * skipbox[rows, cols].astype(jnp.float32)
                inbox[rows, cols] = total.astype(jnp.bfloat16)

            @pl.when(s == half - 1)
            def _():
                gain = gain_ref[pl.ds(gain_row, 1), cols]
                value = inbox[rows, cols].astype(jnp.float32)
                inbox[rows, cols] = (value + gain * value).astype(jnp.bfloat16)

            @pl.loop(0, hidden_width // (4 * tile))
            def _(group):
                for one in range(4):
                    j = group * 4 + one
                    there = pl.ds(pl.multiple_of(j * tile, tile), tile)
                    product = nn(inbox[rows, cols], wo[j, cols, :])
                    if part == 0:
                        acc[:, there] = product
                    elif part < PARTS - 1:
                        acc[:, there] += product
                    else:
                        gu[rows, there] = ((acc[:, there] + product) * slope[rows, there]).astype(jnp.bfloat16)

        first_turn = (s == SECTIONS - 1) & (p == 0)

        @pl.when(first_turn & (c == 1))
        def _():
            pl.semaphore_wait(turn_sem, 1)

        @pl.when(s > 0)
        def _():
            for d in range(CHUNKS):
                @pl.loop(0, chunk // tile)
                def _(k):
                    there = pl.ds(pl.multiple_of(d * chunk + k * tile, tile), tile)
                    grad_x = nn(gu[rows, :], wi[d * (chunk // tile) + k])
                    stage[rows, there] = (inbox[rows, there].astype(jnp.float32) + grad_x).astype(jnp.bfloat16)

                to_next(p, d).start()

        for q in range(PIECES):
            soon = (s == half + 1) & (p == min(q + 1, PIECES - 1))
            @pl.when(soon | ((s > half + 1) & (p == PIECES - 1)))
            def _():
                for d in range(CHUNKS):
                    to_skip(q, d).start()

        @pl.when(first_turn & (c == 0))
        def _():
            pl.semaphore_signal(turn_sem, inc=1, device_id=sibling, device_id_type=MESH)

    for sample in range(tokens // SEQ):
        rows = pl.ds(sample * SEQ, SEQ)
        out_a = nn(gu[rows, :], ph_ref[...])
        out_b = nn(inbox[rows, :], pm_ref[...])

        def outer(a, b):
            return lax.dot_general(
                a, b, (((0,), (0,)), ((), ())), precision=lax.Precision.HIGHEST,
                preferred_element_type=jnp.float32,
            )

        first = outer(in_a[rows, :], out_a)
        second = pltpu.roll(outer(in_b[rows, :], out_b), 64, 1)
        term[sample] = (first[0:64, :] + second[64:128, :]) * (SEQ ** -0.5)

    def last_copy(t, index):
        return pltpu.make_async_remote_copy(
            src_ref=term.at[:, pl.ds(t * 8, 8), :], dst_ref=parts.at[index], send_sem=last_ssem.at[t],
            recv_sem=last_rsem.at[index], device_id=device(t, home_hi, x, c), device_id_type=MESH,
        )

    for t in range(SECTIONS):
        stays = (s == t) & jnp.logical_not(swapped)

        @pl.when(stays)
        def _():
            parts[t] = term[:, t * 8:(t + 1) * 8, :]

        @pl.when(jnp.logical_not(stays))
        def _():
            last_copy(t, s).start()

    for item, pos, there_pos, direction in sends:
        if direction == "core":
            copy_of(item, pos, "core", slab(item, pos, c), sibling).wait_send()
        else:
            copy_of(item, there_pos, "link", source(item, pos, there_pos), toward[direction]).wait_send()

    @pl.when(swapped)
    def _():
        swap_x.wait_send()

    @pl.loop(0, PIECES)
    def _(p):
        for d in range(CHUNKS):
            @pl.when(s > 0)
            def _():
                to_next(p, d).wait_send()

            @pl.when(s > half)
            def _():
                to_skip(p, d).wait_send()

    for t in range(SECTIONS):
        stays = (s == t) & jnp.logical_not(swapped)

        @pl.when(jnp.logical_not(stays))
        def _():
            last_copy(t, s).wait_send()
            last_copy(t, t).wait_recv()

    total = parts[0]
    for t in range(1, SECTIONS):
        total = total + parts[t]
    out_ref[...] = total


def body(saved_inputs, grad_out, w_in, w_out, skip_gain, proj_model, proj_hidden):
    tokens, width = grad_out.shape
    hidden_width = w_in.shape[2]
    samples = tokens // SEQ
    bf16, f32 = jnp.bfloat16, jnp.float32
    dma = pltpu.SemaphoreType.DMA
    result = pl.pallas_call(
        kernel,
        out_shape=jax.ShapeDtypeStruct((samples, 8, 128), f32),
        in_specs=[pl.BlockSpec(memory_space=pl.ANY)] * 4 + [pl.BlockSpec(memory_space=pltpu.VMEM)] * 3,
        out_specs=pl.BlockSpec(memory_space=pltpu.VMEM),
        scratch_shapes=[
            pltpu.VMEM((CHIPS, hidden_width, 256), bf16),
            pltpu.VMEM((2 * CHIPS, width, 256), bf16),
            pltpu.VMEM((tokens, width), bf16),
            pltpu.VMEM((tokens, hidden_width), f32),
            pltpu.VMEM((tokens, width), bf16),
            pltpu.VMEM((tokens, width), bf16),
            pltpu.VMEM((tokens, width), bf16),
            pltpu.VMEM((tokens, hidden_width), bf16),
            pltpu.VMEM((tokens // PIECES, hidden_width), f32),
            pltpu.VMEM((tokens, 128), f32),
            pltpu.VMEM((tokens, 128), f32),
            pltpu.VMEM((samples, 64, 128), f32),
            pltpu.VMEM((SECTIONS, samples, 8, 128), f32),
            dma((4,)),
            dma((len(EVENTS),)),
            dma((len(EVENTS),)),
            dma,
            dma,
            dma((PIECES, CHUNKS)),
            dma((PIECES, CHUNKS)),
            dma((PIECES, CHUNKS)),
            dma((PIECES, CHUNKS)),
            dma((SECTIONS,)),
            dma((SECTIONS,)),
            pltpu.SemaphoreType.REGULAR,
        ],
        compiler_params=pltpu.CompilerParams(
            collective_id=0, has_side_effects=True, vmem_limit_bytes=62 * 2**20
        ),
    )(saved_inputs, grad_out, w_in, w_out, skip_gain, proj_model[0], proj_hidden[0])
    return result[:, :, :64].reshape(samples, 512)


def solution(mesh):
    placed = (
        P("section", "shard", None),
        P("shard", None),
        P("section", "shard", None),
        P("section", "shard", None),
        P(),
        P("section", None, None),
        P("section", None, None),
    )
    return jax.shard_map(
        body, mesh=mesh, in_specs=placed, out_specs=P("shard", "section"), check_vma=False
    )
```

```python
import functools
import math

import jax
import jax.numpy as jnp
from jax import lax
from jax.experimental import pallas as pl
from jax.experimental.pallas import tpu as pltpu
from jax.sharding import PartitionSpec as P

MESH = pl.DeviceIdType.MESH
SEQ = 256
SECTIONS = 8
CHIPS = 8
PIECES = 4
CHUNKS = 4
PARTS = 2
square_root_half = 1.0 / math.sqrt(2.0)
inv_root_two_pi = 1.0 / math.sqrt(2.0 * math.pi)

POSITIONS = ("own", "xm", "xp", "x2a", "x2b", "yo", "pm", "pp", "p2a", "p2b")
ITEMS = (
    ("in", 0, 1792, False),
    ("in", 1792, 2304, True),
    ("out", 0, 896, False),
    ("out", 896, 1152, True),
)
EVENTS = {}
for _item in range(len(ITEMS)):
    for _pos in POSITIONS:
        if _pos != "own":
            EVENTS[(_item, _pos, "link")] = len(EVENTS)
        EVENTS[(_item, _pos, "core")] = len(EVENTS)


EARLY = (
    (0, "own"), (1, "own"), "rest",
    (0, "xm"), (0, "xp"), (1, "yo"), (1, "xm"), (1, "xp"), (0, "yo"), (0, "x2a"), (0, "x2b"),
    (2, "own"), (3, "own"), "swap",
    (1, "pm"), (1, "pp"), (0, "pm"), (0, "pp"), (1, "x2a"), (1, "x2b"), (2, "xm"), (2, "xp"),
    (0, "p2a"), (0, "p2b"), (1, "p2a"), (1, "p2b"),
)
LATE = (
    (3, "yo"), (3, "xm"), (3, "xp"), (2, "yo"), (2, "x2a"), (2, "x2b"), (3, "pm"), (3, "pp"),
    (2, "pm"), (2, "pp"), (3, "x2a"), (3, "x2b"), (2, "p2a"), (2, "p2b"), (3, "p2a"), (3, "p2b"),
)
LAST = 4


def forwards(pos, y_first):
    table = {
        "own": [("xm", "right"), ("xp", "left"), ("yo", "across")],
        "xm": [("x2a", "right")],
        "xp": [("x2b", "left")],
        "x2a": [],
        "x2b": [],
        "yo": [],
        "pm": [],
        "pp": [],
        "p2a": [],
        "p2b": [],
    }
    if y_first:
        table["yo"] = [("pm", "right"), ("pp", "left")]
        table["pm"] = [("p2a", "right")]
        table["pp"] = [("p2b", "left")]
    else:
        table["xm"] = table["xm"] + [("pm", "across")]
        table["xp"] = table["xp"] + [("pp", "across")]
        table["x2a"] = [("p2a", "across")]
        table["x2b"] = [("p2b", "across")]
    return table[pos]


def gelu_parts(value):
    cumulative = 0.5 * (1.0 + lax.erf(value * square_root_half))
    density = jnp.exp(-0.5 * value * value) * inv_root_two_pi
    return (value * cumulative, cumulative + value * density)


def nt(a, b):
    return lax.dot_general(a, b, (((1,), (1,)), ((), ())), preferred_element_type=jnp.float32)


def nn(a, b):
    return jnp.dot(a, b, preferred_element_type=jnp.float32)


def kernel(
    x_ref, g_ref, wi_ref, wo_ref, gain_ref, pm_hbm, ph_hbm, out_ref,
    wi, wo, xs, slope, inbox, skipbox, stage, gu, acc, in_a, in_b, term, parts,
    load_sem, ssem, rsem, swap_ssem, swap_rsem,
    next_ssem, next_rsem, skip_ssem, skip_rsem, last_ssem, last_rsem, turn_sem, pm_ref, ph_ref,
):
    s = lax.axis_index("section")
    h = lax.axis_index("shard")
    yh, x, c = h // 8, (h // 2) % 4, h % 2

    def crosses(section):
        return (lax.rem(section, 2) == 0) & (section < SECTIONS - 2)

    tokens, width = xs.shape
    hidden_width = slope.shape[1]
    piece = tokens // PIECES
    samples = tokens // SEQ
    chunk = width // CHUNKS
    tile = 256

    def device(section, hi, xx, core):
        return (section, hi * 8 + xx * 2 + core)

    right = device(s, yh, (x + 1) % 4, c)
    left = device(s, yh, (x + 3) % 4, c)
    across = device(s, 1 - yh, x, c)
    sibling = device(s, yh, x, 1 - c)
    swapped = crosses(s) & (c == 1)

    def facing(section):
        cross = (crosses(s) | crosses(section)) & (c == 1)
        return device(section, jnp.where(cross, 1 - yh, yh), x, c)

    below = facing(jnp.maximum(s - 1, 0))
    mirror = facing(SECTIONS - 1 - s)
    home_hi = jnp.where(swapped, 1 - yh, yh)
    toward = {"right": right, "left": left, "across": across}

    barrier = pltpu.get_barrier_semaphore()
    for there in (right, left, sibling, across):
        pl.semaphore_signal(barrier, inc=1, device_id=there, device_id_type=MESH)
    for step in range(1, SECTIONS):
        for hi in range(2):
            pl.semaphore_signal(
                barrier, inc=1, device_id=device((s + step) % SECTIONS, hi, x, c), device_id_type=MESH
            )

    own_chip = yh * 4 + x
    slab_in, slab_out = wi_ref.shape[1], wo_ref.shape[1]
    load_in = pltpu.make_async_copy(wi_ref.at[0], gu.at[pl.ds(0, slab_in)], load_sem.at[0])
    load_out = pltpu.make_async_copy(wo_ref.at[0], stage.at[pl.ds(0, slab_out)], load_sem.at[1])
    load_x = pltpu.make_async_copy(x_ref.at[0], xs, load_sem.at[2])
    load_g = pltpu.make_async_copy(g_ref, inbox, load_sem.at[3])
    load_pm = pltpu.make_async_copy(pm_hbm.at[0], pm_ref, load_sem.at[4])
    load_ph = pltpu.make_async_copy(ph_hbm.at[0], ph_ref, load_sem.at[5])
    load_in.start()
    load_out.start()
    load_pm.start()
    load_ph.start()
    @pl.when(jnp.logical_not(swapped))
    def _():
        load_x.start()

    @pl.when(s == SECTIONS - 1)
    def _():
        load_g.start()

    load_in.wait()
    own_cols = pl.ds(pl.multiple_of(c * slab_in, slab_in), slab_in)
    for first in range(0, hidden_width, 512):
        wi[own_chip, first:first + 512, own_cols] = gu[0:slab_in, first:first + 512].T
    pl.semaphore_wait(barrier, 4 + 2 * (SECTIONS - 1))

    def slab(item, pos, core):
        array, first, rows, _ = ITEMS[item]
        hi = yh if pos in ("own", "xm", "xp", "x2a", "x2b") else 1 - yh
        step = {"own": 0, "yo": 0, "xm": 3, "pm": 3, "xp": 1, "pp": 1}.get(pos, 2)
        half = pos[-1] if pos[-1] in "ab" else ""
        return slab_at(array, hi * 4 + (x + step) % 4, core, first, rows, half)

    def slab_at(array, chip, core, first, rows, half):
        if half:
            rows = rows // 2
            first = first + (rows if half == "b" else 0)
        if array == "in":
            return wi.at[chip, pl.ds(first, rows), pl.ds(pl.multiple_of(core * 128, 128), 128)]
        return wo.at[chip * 2 + core, pl.ds(first, rows), :]

    def copy_of(item, pos, kind, src, there):
        event = EVENTS[(item, pos, kind)]
        return pltpu.make_async_remote_copy(
            src_ref=src, dst_ref=src, send_sem=ssem.at[event], recv_sem=rsem.at[event],
            device_id=there, device_id_type=MESH,
        )

    def source(item, pos, there_pos):
        array, first, rows, _ = ITEMS[item]
        half = there_pos[-1] if there_pos[-1] in "ab" else ""
        hi = yh if pos in ("own", "xm", "xp", "x2a", "x2b") else 1 - yh
        step = {"own": 0, "yo": 0, "xm": 3, "pm": 3, "xp": 1, "pp": 1}.get(pos, 2)
        return slab_at(array, hi * 4 + (x + step) % 4, c, first, rows, half)

    sends = []

    def pass_on(item, pos):
        for there_pos, direction in forwards(pos, ITEMS[item][3]):
            cp = copy_of(item, there_pos, "link", source(item, pos, there_pos), toward[direction])
            cp.start()
            sends.append((item, pos, there_pos, direction))
        cp = copy_of(item, pos, "core", slab(item, pos, c), sibling)
        cp.start()
        sends.append((item, pos, pos, "core"))

    def receive(item, pos):
        copy_of(item, pos, "link", slab(item, pos, c), sibling).wait_recv()
        pass_on(item, pos)

    def receive_core(item, pos):
        copy_of(item, pos, "core", slab(item, pos, 1 - c), sibling).wait_recv()

    swap_x = pltpu.make_async_remote_copy(
        src_ref=x_ref.at[0], dst_ref=xs, send_sem=swap_ssem, recv_sem=swap_rsem, device_id=across, device_id_type=MESH
    )
    for entry in EARLY:
        if entry == "swap":
            @pl.when(swapped)
            def _():
                swap_x.start()
        elif entry == "rest":
            load_out.wait()
            for first in range(0, width, 512):
                wo[h, first:first + 512, :] = stage[0:slab_out, first:first + 512].T
        elif entry[1] == "own":
            pass_on(*entry)
        else:
            receive(*entry)
    for item in (0, 1):
        for pos in POSITIONS:
            receive_core(item, pos)

    @pl.when(swapped)
    def _():
        swap_x.wait_recv()

    @pl.when(jnp.logical_not(swapped))
    def _():
        load_x.wait()

    @pl.when(s == SECTIONS - 1)
    def _():
        load_g.wait()

    load_pm.wait()
    load_ph.wait()

    in_a[...] = nn(xs[...], pm_ref[...])
    in_b[...] = jnp.zeros_like(in_b)
    steps = hidden_width // tile

    @pl.loop(0, steps)
    def _(i):
        for at, (item, pos) in enumerate(LATE[:-LAST]):
            @pl.when(i == at * steps // len(LATE[:-LAST]))
            def _():
                receive(item, pos)

        cols = pl.ds(pl.multiple_of(i * tile, tile), tile)
        for part in range(tokens // 256):
            rows = pl.ds(part * 256, 256)
            u = nt(xs[rows, 0:tile], wi[0, cols, :])
            for chip in range(1, CHIPS):
                u = u + nt(xs[rows, chip * tile:(chip + 1) * tile], wi[chip, cols, :])
            act, slant = gelu_parts(u)
            slope[rows, cols] = slant
            in_b[rows, :] += nn(act.astype(jnp.bfloat16), ph_ref[cols, :])

    for item, pos in LATE[-LAST:]:
        receive(item, pos)
    for item in (2, 3):
        for pos in POSITIONS:
            receive_core(item, pos)

    def chunk_copy(p, d, src, dst, send, recv, there):
        where = (pl.ds(pl.multiple_of(p * piece, piece), piece), pl.ds(d * chunk, chunk))
        return pltpu.make_async_remote_copy(
            src_ref=src.at[where], dst_ref=dst.at[where], send_sem=send.at[p, d], recv_sem=recv.at[p, d],
            device_id=there, device_id_type=MESH,
        )

    def to_next(p, d):
        return chunk_copy(p, d, stage, inbox, next_ssem, next_rsem, below)

    def to_skip(p, d):
        return chunk_copy(p, d, stage, skipbox, skip_ssem, skip_rsem, mirror)

    def outer(a, b):
        return lax.dot_general(
            a, b, (((0,), (0,)), ((), ())), precision=lax.Precision.HIGHEST,
            preferred_element_type=jnp.float32,
        )

    def last_copy(t, sample, index):
        return pltpu.make_async_remote_copy(
            src_ref=term.at[sample, pl.ds(t * 8, 8), :], dst_ref=parts.at[index, sample],
            send_sem=last_ssem.at[t, sample], recv_sem=last_rsem.at[index, sample],
            device_id=device(t, home_hi, x, c), device_id_type=MESH,
        )

    def finish(sample):
        rows = pl.ds(sample * SEQ, SEQ)
        out_a = nn(gu[rows, :], ph_ref[...])
        out_b = nn(inbox[rows, :], pm_ref[...])
        first = outer(in_a[rows, :], out_a)
        second = pltpu.roll(outer(in_b[rows, :], out_b), 64, 1)
        term[sample] = (first[0:64, :] + second[64:128, :]) * (SEQ ** -0.5)
        for t in range(SECTIONS):
            stays = (s == t) & jnp.logical_not(swapped)

            @pl.when(stays)
            def _():
                parts[t, sample] = term[sample, t * 8:(t + 1) * 8, :]

            @pl.when(jnp.logical_not(stays))
            def _():
                last_copy(t, sample, s).start()

    half = SECTIONS // 2
    gain_row = jnp.clip(half - 1 - s, 0, half - 1)

    @pl.loop(0, PIECES)
    def _(p):
        rows = pl.ds(pl.multiple_of(p * piece, piece), piece)
        for part in range(PARTS):
            cols = pl.ds(part * (width // PARTS), width // PARTS)
            chunks = range(part * CHUNKS // PARTS, (part + 1) * CHUNKS // PARTS)

            @pl.when(s < SECTIONS - 1)
            def _():
                for d in chunks:
                    to_next(p, d).wait_recv()

            @pl.when(s < half - 1)
            def _():
                for d in chunks:
                    to_skip(p, d).wait_recv()
                gain = gain_ref[pl.ds(gain_row, 1), cols]
                total = inbox[rows, cols].astype(jnp.float32) + gain * skipbox[rows, cols].astype(jnp.float32)
                inbox[rows, cols] = total.astype(jnp.bfloat16)

            @pl.when(s == half - 1)
            def _():
                gain = gain_ref[pl.ds(gain_row, 1), cols]
                value = inbox[rows, cols].astype(jnp.float32)
                inbox[rows, cols] = (value + gain * value).astype(jnp.bfloat16)

            @pl.loop(0, hidden_width // (4 * tile))
            def _(group):
                for one in range(4):
                    j = group * 4 + one
                    there = pl.ds(pl.multiple_of(j * tile, tile), tile)
                    product = nn(inbox[rows, cols], wo[j, cols, :])
                    if part == 0:
                        acc[:, there] = product
                    elif part < PARTS - 1:
                        acc[:, there] += product
                    else:
                        gu[rows, there] = ((acc[:, there] + product) * slope[rows, there]).astype(jnp.bfloat16)

        first_turn = (s == SECTIONS - 1) & (p == 0)

        @pl.when(first_turn & (c == 1))
        def _():
            pl.semaphore_wait(turn_sem, 1)

        @pl.when(s > 0)
        def _():
            for d in range(CHUNKS):
                @pl.loop(0, chunk // tile)
                def _(k):
                    there = pl.ds(pl.multiple_of(d * chunk + k * tile, tile), tile)
                    grad_x = nn(gu[rows, :], wi[d * (chunk // tile) + k])
                    stage[rows, there] = (inbox[rows, there].astype(jnp.float32) + grad_x).astype(jnp.bfloat16)

                to_next(p, d).start()

        for q in range(PIECES):
            soon = (s == half + 1) & (p == min(q + 1, PIECES - 1))
            @pl.when(soon | ((s > half + 1) & (p == PIECES - 1)))
            def _():
                for d in range(CHUNKS):
                    to_skip(q, d).start()

        for sample in range(samples - 1):
            @pl.when(p == (sample + 1) * SEQ // piece - 1)
            def _():
                finish(sample)

        @pl.when(first_turn & (c == 0))
        def _():
            pl.semaphore_signal(turn_sem, inc=1, device_id=sibling, device_id_type=MESH)

    finish(samples - 1)

    for item, pos, there_pos, direction in sends:
        if direction == "core":
            copy_of(item, pos, "core", slab(item, pos, c), sibling).wait_send()
        else:
            copy_of(item, there_pos, "link", source(item, pos, there_pos), toward[direction]).wait_send()

    @pl.when(swapped)
    def _():
        swap_x.wait_send()

    @pl.loop(0, PIECES)
    def _(p):
        for d in range(CHUNKS):
            @pl.when(s > 0)
            def _():
                to_next(p, d).wait_send()

            @pl.when(s > half)
            def _():
                to_skip(p, d).wait_send()

    for t in range(SECTIONS):
        stays = (s == t) & jnp.logical_not(swapped)

        @pl.when(jnp.logical_not(stays))
        def _():
            for sample in range(samples):
                last_copy(t, sample, s).wait_send()
                last_copy(t, sample, t).wait_recv()

    total = parts[0]
    for t in range(1, SECTIONS):
        total = total + parts[t]
    out_ref[...] = total


def body(saved_inputs, grad_out, w_in, w_out, skip_gain, proj_model, proj_hidden):
    tokens, width = grad_out.shape
    hidden_width = w_in.shape[2]
    samples = tokens // SEQ
    bf16, f32 = jnp.bfloat16, jnp.float32
    dma = pltpu.SemaphoreType.DMA
    result = pl.pallas_call(
        kernel,
        out_shape=jax.ShapeDtypeStruct((samples, 8, 128), f32),
        in_specs=[pl.BlockSpec(memory_space=pl.ANY)] * 4 + [pl.BlockSpec(memory_space=pltpu.VMEM)] + [pl.BlockSpec(memory_space=pl.ANY)] * 2,
        out_specs=pl.BlockSpec(memory_space=pltpu.VMEM),
        scratch_shapes=[
            pltpu.VMEM((CHIPS, hidden_width, 256), bf16),
            pltpu.VMEM((2 * CHIPS, width, 256), bf16),
            pltpu.VMEM((tokens, width), bf16),
            pltpu.VMEM((tokens, hidden_width), f32),
            pltpu.VMEM((tokens, width), bf16),
            pltpu.VMEM((tokens, width), bf16),
            pltpu.VMEM((tokens, width), bf16),
            pltpu.VMEM((tokens, hidden_width), bf16),
            pltpu.VMEM((tokens // PIECES, hidden_width), f32),
            pltpu.VMEM((tokens, 128), f32),
            pltpu.VMEM((tokens, 128), f32),
            pltpu.VMEM((samples, 64, 128), f32),
            pltpu.VMEM((SECTIONS, samples, 8, 128), f32),
            dma((6,)),
            dma((len(EVENTS),)),
            dma((len(EVENTS),)),
            dma,
            dma,
            dma((PIECES, CHUNKS)),
            dma((PIECES, CHUNKS)),
            dma((PIECES, CHUNKS)),
            dma((PIECES, CHUNKS)),
            dma((SECTIONS, samples)),
            dma((SECTIONS, samples)),
            pltpu.SemaphoreType.REGULAR,
            pltpu.VMEM(proj_model.shape[1:], bf16),
            pltpu.VMEM(proj_hidden.shape[1:], bf16),
        ],
        compiler_params=pltpu.CompilerParams(
            collective_id=0, has_side_effects=True, vmem_limit_bytes=62 * 2**20
        ),
    )(saved_inputs, grad_out, w_in, w_out, skip_gain, proj_model, proj_hidden)
    return result[:, :, :64].reshape(samples, 512)


def solution(mesh):
    placed = (
        P("section", "shard", None),
        P("shard", None),
        P("section", "shard", None),
        P("section", "shard", None),
        P(),
        P("section", None, None),
        P("section", None, None),
    )
    return jax.shard_map(
        body, mesh=mesh, in_specs=placed, out_specs=P("shard", "section"), check_vma=False
    )
```

```python
import functools
import math

import jax
import jax.numpy as jnp
from jax import lax
from jax.experimental import pallas as pl
from jax.experimental.pallas import tpu as pltpu
from jax.sharding import PartitionSpec as P

MESH = pl.DeviceIdType.MESH
SEQ = 256
SECTIONS = 8
CHIPS = 8
PIECES = 4
CHUNKS = 4
PARTS = 2
square_root_half = 1.0 / math.sqrt(2.0)
inv_root_two_pi = 1.0 / math.sqrt(2.0 * math.pi)

POSITIONS = ("own", "xm", "xp", "x2a", "x2b", "yo", "pm", "pp", "p2a", "p2b")
ITEMS = (
    ("in", 0, 1856, False),
    ("in", 1856, 2240, True),
    ("out", 0, 928, False),
    ("out", 928, 1120, True),
)
EVENTS = {}
for _item in range(len(ITEMS)):
    for _pos in POSITIONS:
        if _pos != "own":
            EVENTS[(_item, _pos, "link")] = len(EVENTS)
        EVENTS[(_item, _pos, "core")] = len(EVENTS)


EARLY = (
    (0, "own"), (1, "own"), "rest",
    (0, "xm"), (0, "xp"), (1, "yo"), (1, "xm"), (1, "xp"), (0, "yo"), (0, "x2a"), (0, "x2b"),
    (2, "own"), (3, "own"), "swap",
    (1, "pm"), (1, "pp"), (0, "pm"), (0, "pp"), (1, "x2a"), (1, "x2b"), (2, "xm"), (2, "xp"),
    (0, "p2a"), (0, "p2b"), (1, "p2a"), (1, "p2b"),
)
LATE = (
    (3, "yo"), (3, "xm"), (3, "xp"), (2, "yo"), (2, "x2a"), (2, "x2b"), (3, "pm"), (3, "pp"),
    (2, "pm"), (2, "pp"), (3, "x2a"), (3, "x2b"), (2, "p2a"), (2, "p2b"), (3, "p2a"), (3, "p2b"),
)
LAST = 4


def forwards(pos, y_first):
    table = {
        "own": [("xm", "right"), ("xp", "left"), ("yo", "across")],
        "xm": [("x2a", "right")],
        "xp": [("x2b", "left")],
        "x2a": [],
        "x2b": [],
        "yo": [],
        "pm": [],
        "pp": [],
        "p2a": [],
        "p2b": [],
    }
    if y_first:
        table["yo"] = [("pm", "right"), ("pp", "left")]
        table["pm"] = [("p2a", "right")]
        table["pp"] = [("p2b", "left")]
    else:
        table["xm"] = table["xm"] + [("pm", "across")]
        table["xp"] = table["xp"] + [("pp", "across")]
        table["x2a"] = [("p2a", "across")]
        table["x2b"] = [("p2b", "across")]
    return table[pos]


def gelu_parts(value):
    cumulative = 0.5 * (1.0 + lax.erf(value * square_root_half))
    density = jnp.exp(-0.5 * value * value) * inv_root_two_pi
    return (value * cumulative, cumulative + value * density)


def nt(a, b):
    return lax.dot_general(a, b, (((1,), (1,)), ((), ())), preferred_element_type=jnp.float32)


def nn(a, b):
    return jnp.dot(a, b, preferred_element_type=jnp.float32)


def kernel(
    x_ref, g_ref, wi_ref, wo_ref, gain_ref, pm_hbm, ph_hbm, out_ref,
    wi, wo, xs, slope, inbox, skipbox, stage, gu, acc, in_a, in_b, term, parts,
    load_sem, ssem, rsem, swap_ssem, swap_rsem,
    next_ssem, next_rsem, skip_ssem, skip_rsem, last_ssem, last_rsem, turn_sem, pm_ref, ph_ref,
):
    s = lax.axis_index("section")
    h = lax.axis_index("shard")
    yh, x, c = h // 8, (h // 2) % 4, h % 2

    def crosses(section):
        return (lax.rem(section, 2) == 0) & (section < SECTIONS - 2)

    tokens, width = xs.shape
    hidden_width = slope.shape[1]
    piece = tokens // PIECES
    samples = tokens // SEQ
    chunk = width // CHUNKS
    tile = 256

    def device(section, hi, xx, core):
        return (section, hi * 8 + xx * 2 + core)

    right = device(s, yh, (x + 1) % 4, c)
    left = device(s, yh, (x + 3) % 4, c)
    across = device(s, 1 - yh, x, c)
    sibling = device(s, yh, x, 1 - c)
    swapped = crosses(s) & (c == 1)

    def facing(section):
        cross = (crosses(s) | crosses(section)) & (c == 1)
        return device(section, jnp.where(cross, 1 - yh, yh), x, c)

    below = facing(jnp.maximum(s - 1, 0))
    mirror = facing(SECTIONS - 1 - s)
    home_hi = jnp.where(swapped, 1 - yh, yh)
    toward = {"right": right, "left": left, "across": across}

    barrier = pltpu.get_barrier_semaphore()
    for there in (right, left, sibling, across):
        pl.semaphore_signal(barrier, inc=1, device_id=there, device_id_type=MESH)
    for step in range(1, SECTIONS):
        for hi in range(2):
            pl.semaphore_signal(
                barrier, inc=1, device_id=device((s + step) % SECTIONS, hi, x, c), device_id_type=MESH
            )

    own_chip = yh * 4 + x
    slab_in, slab_out = wi_ref.shape[1], wo_ref.shape[1]
    load_in = pltpu.make_async_copy(wi_ref.at[0], gu.at[pl.ds(0, slab_in)], load_sem.at[0])
    load_out = pltpu.make_async_copy(wo_ref.at[0], stage.at[pl.ds(0, slab_out)], load_sem.at[1])
    load_x = pltpu.make_async_copy(x_ref.at[0], xs, load_sem.at[2])
    load_g = pltpu.make_async_copy(g_ref, inbox, load_sem.at[3])
    load_pm = pltpu.make_async_copy(pm_hbm.at[0], pm_ref, load_sem.at[4])
    load_ph = pltpu.make_async_copy(ph_hbm.at[0], ph_ref, load_sem.at[5])
    load_in.start()
    load_out.start()
    load_pm.start()
    load_ph.start()
    @pl.when(jnp.logical_not(swapped))
    def _():
        load_x.start()

    @pl.when(s == SECTIONS - 1)
    def _():
        load_g.start()

    load_in.wait()
    own_cols = pl.ds(pl.multiple_of(c * slab_in, slab_in), slab_in)
    for first in range(0, hidden_width, 512):
        wi[own_chip, first:first + 512, own_cols] = gu[0:slab_in, first:first + 512].T
    pl.semaphore_wait(barrier, 4 + 2 * (SECTIONS - 1))

    def slab(item, pos, core):
        array, first, rows, _ = ITEMS[item]
        hi = yh if pos in ("own", "xm", "xp", "x2a", "x2b") else 1 - yh
        step = {"own": 0, "yo": 0, "xm": 3, "pm": 3, "xp": 1, "pp": 1}.get(pos, 2)
        half = pos[-1] if pos[-1] in "ab" else ""
        return slab_at(array, hi * 4 + (x + step) % 4, core, first, rows, half)

    def slab_at(array, chip, core, first, rows, half):
        if half:
            rows = rows // 2
            first = first + (rows if half == "b" else 0)
        if array == "in":
            return wi.at[chip, pl.ds(first, rows), pl.ds(pl.multiple_of(core * 128, 128), 128)]
        return wo.at[chip * 2 + core, pl.ds(first, rows), :]

    def copy_of(item, pos, kind, src, there):
        event = EVENTS[(item, pos, kind)]
        return pltpu.make_async_remote_copy(
            src_ref=src, dst_ref=src, send_sem=ssem.at[event], recv_sem=rsem.at[event],
            device_id=there, device_id_type=MESH,
        )

    def source(item, pos, there_pos):
        array, first, rows, _ = ITEMS[item]
        half = there_pos[-1] if there_pos[-1] in "ab" else ""
        hi = yh if pos in ("own", "xm", "xp", "x2a", "x2b") else 1 - yh
        step = {"own": 0, "yo": 0, "xm": 3, "pm": 3, "xp": 1, "pp": 1}.get(pos, 2)
        return slab_at(array, hi * 4 + (x + step) % 4, c, first, rows, half)

    sends = []

    def pass_on(item, pos):
        for there_pos, direction in forwards(pos, ITEMS[item][3]):
            cp = copy_of(item, there_pos, "link", source(item, pos, there_pos), toward[direction])
            cp.start()
            sends.append((item, pos, there_pos, direction))
        cp = copy_of(item, pos, "core", slab(item, pos, c), sibling)
        cp.start()
        sends.append((item, pos, pos, "core"))

    def receive(item, pos):
        copy_of(item, pos, "link", slab(item, pos, c), sibling).wait_recv()
        pass_on(item, pos)

    def receive_core(item, pos):
        copy_of(item, pos, "core", slab(item, pos, 1 - c), sibling).wait_recv()

    swap_x = pltpu.make_async_remote_copy(
        src_ref=x_ref.at[0], dst_ref=xs, send_sem=swap_ssem, recv_sem=swap_rsem, device_id=across, device_id_type=MESH
    )
    for entry in EARLY:
        if entry == "swap":
            @pl.when(swapped)
            def _():
                swap_x.start()
        elif entry == "rest":
            load_out.wait()
            for first in range(0, width, 512):
                wo[h, first:first + 512, :] = stage[0:slab_out, first:first + 512].T
        elif entry[1] == "own":
            pass_on(*entry)
        else:
            receive(*entry)
    for item in (0, 1):
        for pos in POSITIONS:
            receive_core(item, pos)

    @pl.when(swapped)
    def _():
        swap_x.wait_recv()

    @pl.when(jnp.logical_not(swapped))
    def _():
        load_x.wait()

    @pl.when(s == SECTIONS - 1)
    def _():
        load_g.wait()

    load_pm.wait()
    load_ph.wait()

    in_a[...] = nn(xs[...], pm_ref[...])
    in_b[...] = jnp.zeros_like(in_b)
    steps = hidden_width // tile

    @pl.loop(0, steps)
    def _(i):
        for at, (item, pos) in enumerate(LATE[:-LAST]):
            @pl.when(i == at * steps // len(LATE[:-LAST]))
            def _():
                receive(item, pos)

        cols = pl.ds(pl.multiple_of(i * tile, tile), tile)
        for part in range(tokens // 256):
            rows = pl.ds(part * 256, 256)
            u = nt(xs[rows, 0:tile], wi[0, cols, :])
            for chip in range(1, CHIPS):
                u = u + nt(xs[rows, chip * tile:(chip + 1) * tile], wi[chip, cols, :])
            act, slant = gelu_parts(u)
            slope[rows, cols] = slant
            in_b[rows, :] += nn(act.astype(jnp.bfloat16), ph_ref[cols, :])

    for item, pos in LATE[-LAST:]:
        receive(item, pos)
    for item in (2, 3):
        for pos in POSITIONS:
            receive_core(item, pos)

    def chunk_copy(p, d, src, dst, send, recv, there):
        where = (pl.ds(pl.multiple_of(p * piece, piece), piece), pl.ds(d * chunk, chunk))
        return pltpu.make_async_remote_copy(
            src_ref=src.at[where], dst_ref=dst.at[where], send_sem=send.at[p, d], recv_sem=recv.at[p, d],
            device_id=there, device_id_type=MESH,
        )

    def to_next(p, d):
        return chunk_copy(p, d, stage, inbox, next_ssem, next_rsem, below)

    def to_skip(p, d):
        return chunk_copy(p, d, stage, skipbox, skip_ssem, skip_rsem, mirror)

    def outer(a, b):
        return lax.dot_general(
            a, b, (((0,), (0,)), ((), ())), precision=lax.Precision.HIGHEST,
            preferred_element_type=jnp.float32,
        )

    def last_copy(t, sample, index):
        return pltpu.make_async_remote_copy(
            src_ref=term.at[sample, pl.ds(t * 8, 8), :], dst_ref=parts.at[index, sample],
            send_sem=last_ssem.at[t, sample], recv_sem=last_rsem.at[index, sample],
            device_id=device(t, home_hi, x, c), device_id_type=MESH,
        )

    def finish(sample):
        rows = pl.ds(sample * SEQ, SEQ)
        out_a = nn(gu[rows, :], ph_ref[...])
        out_b = nn(inbox[rows, :], pm_ref[...])
        first = outer(in_a[rows, :], out_a)
        second = pltpu.roll(outer(in_b[rows, :], out_b), 64, 1)
        term[sample] = (first[0:64, :] + second[64:128, :]) * (SEQ ** -0.5)
        for t in range(SECTIONS):
            stays = (s == t) & jnp.logical_not(swapped)

            @pl.when(stays)
            def _():
                parts[t, sample] = term[sample, t * 8:(t + 1) * 8, :]

            @pl.when(jnp.logical_not(stays))
            def _():
                last_copy(t, sample, s).start()

    half = SECTIONS // 2
    gain_row = jnp.clip(half - 1 - s, 0, half - 1)

    @pl.loop(0, PIECES)
    def _(p):
        rows = pl.ds(pl.multiple_of(p * piece, piece), piece)
        for part in range(PARTS):
            cols = pl.ds(part * (width // PARTS), width // PARTS)
            chunks = range(part * CHUNKS // PARTS, (part + 1) * CHUNKS // PARTS)

            @pl.when(s < SECTIONS - 1)
            def _():
                for d in chunks:
                    to_next(p, d).wait_recv()

            @pl.when(s < half - 1)
            def _():
                for d in chunks:
                    to_skip(p, d).wait_recv()
                gain = gain_ref[pl.ds(gain_row, 1), cols]
                total = inbox[rows, cols].astype(jnp.float32) + gain * skipbox[rows, cols].astype(jnp.float32)
                inbox[rows, cols] = total.astype(jnp.bfloat16)

            @pl.when(s == half - 1)
            def _():
                gain = gain_ref[pl.ds(gain_row, 1), cols]
                value = inbox[rows, cols].astype(jnp.float32)
                inbox[rows, cols] = (value + gain * value).astype(jnp.bfloat16)

            @pl.loop(0, hidden_width // (4 * tile))
            def _(group):
                for one in range(4):
                    j = group * 4 + one
                    there = pl.ds(pl.multiple_of(j * tile, tile), tile)
                    product = nn(inbox[rows, cols], wo[j, cols, :])
                    if part == 0:
                        acc[:, there] = product
                    elif part < PARTS - 1:
                        acc[:, there] += product
                    else:
                        gu[rows, there] = ((acc[:, there] + product) * slope[rows, there]).astype(jnp.bfloat16)

        first_turn = (s == SECTIONS - 1) & (p == 0)

        @pl.when(first_turn & (c == 1))
        def _():
            pl.semaphore_wait(turn_sem, 1)

        @pl.when(s > 0)
        def _():
            for d in range(CHUNKS):
                @pl.loop(0, chunk // tile)
                def _(k):
                    there = pl.ds(pl.multiple_of(d * chunk + k * tile, tile), tile)
                    grad_x = nn(gu[rows, :], wi[d * (chunk // tile) + k])
                    stage[rows, there] = (inbox[rows, there].astype(jnp.float32) + grad_x).astype(jnp.bfloat16)

                to_next(p, d).start()

        for q in range(PIECES):
            soon = (s == half + 1) & (p == min(q + 1, PIECES - 1))
            @pl.when(soon | ((s > half + 1) & (p == PIECES - 1)))
            def _():
                for d in range(CHUNKS):
                    to_skip(q, d).start()

        for sample in range(samples - 1):
            @pl.when(p == (sample + 1) * SEQ // piece - 1)
            def _():
                finish(sample)

        @pl.when(first_turn & (c == 0))
        def _():
            pl.semaphore_signal(turn_sem, inc=1, device_id=sibling, device_id_type=MESH)

    finish(samples - 1)

    for item, pos, there_pos, direction in sends:
        if direction == "core":
            copy_of(item, pos, "core", slab(item, pos, c), sibling).wait_send()
        else:
            copy_of(item, there_pos, "link", source(item, pos, there_pos), toward[direction]).wait_send()

    @pl.when(swapped)
    def _():
        swap_x.wait_send()

    @pl.loop(0, PIECES)
    def _(p):
        for d in range(CHUNKS):
            @pl.when(s > 0)
            def _():
                to_next(p, d).wait_send()

            @pl.when(s > half)
            def _():
                to_skip(p, d).wait_send()

    for t in range(SECTIONS):
        stays = (s == t) & jnp.logical_not(swapped)

        @pl.when(jnp.logical_not(stays))
        def _():
            for sample in range(samples):
                last_copy(t, sample, s).wait_send()
                last_copy(t, sample, t).wait_recv()

    total = parts[0]
    for t in range(1, SECTIONS):
        total = total + parts[t]
    out_ref[...] = total


def body(saved_inputs, grad_out, w_in, w_out, skip_gain, proj_model, proj_hidden):
    tokens, width = grad_out.shape
    hidden_width = w_in.shape[2]
    samples = tokens // SEQ
    bf16, f32 = jnp.bfloat16, jnp.float32
    dma = pltpu.SemaphoreType.DMA
    result = pl.pallas_call(
        kernel,
        out_shape=jax.ShapeDtypeStruct((samples, 8, 128), f32),
        in_specs=[pl.BlockSpec(memory_space=pl.ANY)] * 4 + [pl.BlockSpec(memory_space=pltpu.VMEM)] + [pl.BlockSpec(memory_space=pl.ANY)] * 2,
        out_specs=pl.BlockSpec(memory_space=pltpu.VMEM),
        scratch_shapes=[
            pltpu.VMEM((CHIPS, hidden_width, 256), bf16),
            pltpu.VMEM((2 * CHIPS, width, 256), bf16),
            pltpu.VMEM((tokens, width), bf16),
            pltpu.VMEM((tokens, hidden_width), f32),
            pltpu.VMEM((tokens, width), bf16),
            pltpu.VMEM((tokens, width), bf16),
            pltpu.VMEM((tokens, width), bf16),
            pltpu.VMEM((tokens, hidden_width), bf16),
            pltpu.VMEM((tokens // PIECES, hidden_width), f32),
            pltpu.VMEM((tokens, 128), f32),
            pltpu.VMEM((tokens, 128), f32),
            pltpu.VMEM((samples, 64, 128), f32),
            pltpu.VMEM((SECTIONS, samples, 8, 128), f32),
            dma((6,)),
            dma((len(EVENTS),)),
            dma((len(EVENTS),)),
            dma,
            dma,
            dma((PIECES, CHUNKS)),
            dma((PIECES, CHUNKS)),
            dma((PIECES, CHUNKS)),
            dma((PIECES, CHUNKS)),
            dma((SECTIONS, samples)),
            dma((SECTIONS, samples)),
            pltpu.SemaphoreType.REGULAR,
            pltpu.VMEM(proj_model.shape[1:], bf16),
            pltpu.VMEM(proj_hidden.shape[1:], bf16),
        ],
        compiler_params=pltpu.CompilerParams(
            collective_id=0, has_side_effects=True, vmem_limit_bytes=62 * 2**20
        ),
    )(saved_inputs, grad_out, w_in, w_out, skip_gain, proj_model, proj_hidden)
    return result[:, :, :64].reshape(samples, 512)


def solution(mesh):
    placed = (
        P("section", "shard", None),
        P("shard", None),
        P("section", "shard", None),
        P("section", "shard", None),
        P(),
        P("section", None, None),
        P("section", None, None),
    )
    return jax.shard_map(
        body, mesh=mesh, in_specs=placed, out_specs=P("shard", "section"), check_vma=False
    )
```

```python
import functools
import math

import jax
import jax.numpy as jnp
from jax import lax
from jax.experimental import pallas as pl
from jax.experimental.pallas import tpu as pltpu
from jax.sharding import PartitionSpec as P

MESH = pl.DeviceIdType.MESH
SEQ = 256
SECTIONS = 8
CHIPS = 8
PIECES = 4
CHUNKS = 4
PARTS = 2
square_root_half = 1.0 / math.sqrt(2.0)
inv_root_two_pi = 1.0 / math.sqrt(2.0 * math.pi)

POSITIONS = ("own", "xm", "xp", "x2a", "x2b", "yo", "pm", "pp", "p2a", "p2b")
ITEMS = (
    ("in", 0, 1920, False),
    ("in", 1920, 2176, True),
    ("out", 0, 960, False),
    ("out", 960, 1088, True),
)
EVENTS = {}
for _item in range(len(ITEMS)):
    for _pos in POSITIONS:
        if _pos != "own":
            EVENTS[(_item, _pos, "link")] = len(EVENTS)
        EVENTS[(_item, _pos, "core")] = len(EVENTS)


EARLY = (
    (0, "own"), (1, "own"), "rest",
    (0, "xm"), (0, "xp"), (1, "yo"), (1, "xm"), (1, "xp"), (0, "yo"), (0, "x2a"), (0, "x2b"),
    (2, "own"), (3, "own"), "swap",
    (1, "pm"), (1, "pp"), (0, "pm"), (0, "pp"), (1, "x2a"), (1, "x2b"), (2, "xm"), (2, "xp"),
    (0, "p2a"), (0, "p2b"), (1, "p2a"), (1, "p2b"),
)
LATE = (
    (3, "yo"), (3, "xm"), (3, "xp"), (2, "yo"), (2, "x2a"), (2, "x2b"), (3, "pm"), (3, "pp"),
    (2, "pm"), (2, "pp"), (3, "x2a"), (3, "x2b"), (2, "p2a"), (2, "p2b"), (3, "p2a"), (3, "p2b"),
)
LAST = 4


def forwards(pos, y_first):
    table = {
        "own": [("xm", "right"), ("xp", "left"), ("yo", "across")],
        "xm": [("x2a", "right")],
        "xp": [("x2b", "left")],
        "x2a": [],
        "x2b": [],
        "yo": [],
        "pm": [],
        "pp": [],
        "p2a": [],
        "p2b": [],
    }
    if y_first:
        table["yo"] = [("pm", "right"), ("pp", "left")]
        table["pm"] = [("p2a", "right")]
        table["pp"] = [("p2b", "left")]
    else:
        table["xm"] = table["xm"] + [("pm", "across")]
        table["xp"] = table["xp"] + [("pp", "across")]
        table["x2a"] = [("p2a", "across")]
        table["x2b"] = [("p2b", "across")]
    return table[pos]


def gelu_parts(value):
    cumulative = 0.5 * (1.0 + lax.erf(value * square_root_half))
    density = jnp.exp(-0.5 * value * value) * inv_root_two_pi
    return (value * cumulative, cumulative + value * density)


def nt(a, b):
    return lax.dot_general(a, b, (((1,), (1,)), ((), ())), preferred_element_type=jnp.float32)


def nn(a, b):
    return jnp.dot(a, b, preferred_element_type=jnp.float32)


def kernel(
    x_ref, g_ref, wi_ref, wo_ref, gain_ref, pm_hbm, ph_hbm, out_ref,
    wi, wo, xs, slope, inbox, skipbox, stage, gu, acc, in_a, in_b, term, parts,
    load_sem, ssem, rsem, swap_ssem, swap_rsem,
    next_ssem, next_rsem, skip_ssem, skip_rsem, last_ssem, last_rsem, turn_sem, pm_ref, ph_ref,
):
    s = lax.axis_index("section")
    h = lax.axis_index("shard")
    yh, x, c = h // 8, (h // 2) % 4, h % 2

    def crosses(section):
        return (lax.rem(section, 2) == 0) & (section < SECTIONS - 2)

    tokens, width = xs.shape
    hidden_width = slope.shape[1]
    piece = tokens // PIECES
    samples = tokens // SEQ
    chunk = width // CHUNKS
    tile = 256

    def device(section, hi, xx, core):
        return (section, hi * 8 + xx * 2 + core)

    right = device(s, yh, (x + 1) % 4, c)
    left = device(s, yh, (x + 3) % 4, c)
    across = device(s, 1 - yh, x, c)
    sibling = device(s, yh, x, 1 - c)
    swapped = crosses(s) & (c == 1)

    def facing(section):
        cross = (crosses(s) | crosses(section)) & (c == 1)
        return device(section, jnp.where(cross, 1 - yh, yh), x, c)

    below = facing(jnp.maximum(s - 1, 0))
    mirror = facing(SECTIONS - 1 - s)
    home_hi = jnp.where(swapped, 1 - yh, yh)
    toward = {"right": right, "left": left, "across": across}

    barrier = pltpu.get_barrier_semaphore()
    for there in (right, left, sibling, across):
        pl.semaphore_signal(barrier, inc=1, device_id=there, device_id_type=MESH)
    for step in range(1, SECTIONS):
        for hi in range(2):
            pl.semaphore_signal(
                barrier, inc=1, device_id=device((s + step) % SECTIONS, hi, x, c), device_id_type=MESH
            )

    own_chip = yh * 4 + x
    slab_in, slab_out = wi_ref.shape[1], wo_ref.shape[1]
    load_in = pltpu.make_async_copy(wi_ref.at[0], gu.at[pl.ds(0, slab_in)], load_sem.at[0])
    load_out = pltpu.make_async_copy(wo_ref.at[0], stage.at[pl.ds(0, slab_out)], load_sem.at[1])
    load_x = pltpu.make_async_copy(x_ref.at[0], xs, load_sem.at[2])
    load_g = pltpu.make_async_copy(g_ref, inbox, load_sem.at[3])
    load_pm = pltpu.make_async_copy(pm_hbm.at[0], pm_ref, load_sem.at[4])
    load_ph = pltpu.make_async_copy(ph_hbm.at[0], ph_ref, load_sem.at[5])
    load_in.start()
    load_out.start()
    load_pm.start()
    load_ph.start()
    @pl.when(jnp.logical_not(swapped))
    def _():
        load_x.start()

    @pl.when(s == SECTIONS - 1)
    def _():
        load_g.start()

    load_in.wait()
    own_cols = pl.ds(pl.multiple_of(c * slab_in, slab_in), slab_in)
    for first in range(0, hidden_width, 512):
        wi[own_chip, first:first + 512, own_cols] = gu[0:slab_in, first:first + 512].T
    pl.semaphore_wait(barrier, 4 + 2 * (SECTIONS - 1))

    def slab(item, pos, core):
        array, first, rows, _ = ITEMS[item]
        hi = yh if pos in ("own", "xm", "xp", "x2a", "x2b") else 1 - yh
        step = {"own": 0, "yo": 0, "xm": 3, "pm": 3, "xp": 1, "pp": 1}.get(pos, 2)
        half = pos[-1] if pos[-1] in "ab" else ""
        return slab_at(array, hi * 4 + (x + step) % 4, core, first, rows, half)

    def slab_at(array, chip, core, first, rows, half):
        if half:
            rows = rows // 2
            first = first + (rows if half == "b" else 0)
        if array == "in":
            return wi.at[chip, pl.ds(first, rows), pl.ds(pl.multiple_of(core * 128, 128), 128)]
        return wo.at[chip * 2 + core, pl.ds(first, rows), :]

    def copy_of(item, pos, kind, src, there):
        event = EVENTS[(item, pos, kind)]
        return pltpu.make_async_remote_copy(
            src_ref=src, dst_ref=src, send_sem=ssem.at[event], recv_sem=rsem.at[event],
            device_id=there, device_id_type=MESH,
        )

    def source(item, pos, there_pos):
        array, first, rows, _ = ITEMS[item]
        half = there_pos[-1] if there_pos[-1] in "ab" else ""
        hi = yh if pos in ("own", "xm", "xp", "x2a", "x2b") else 1 - yh
        step = {"own": 0, "yo": 0, "xm": 3, "pm": 3, "xp": 1, "pp": 1}.get(pos, 2)
        return slab_at(array, hi * 4 + (x + step) % 4, c, first, rows, half)

    sends = []

    def pass_on(item, pos):
        for there_pos, direction in forwards(pos, ITEMS[item][3]):
            cp = copy_of(item, there_pos, "link", source(item, pos, there_pos), toward[direction])
            cp.start()
            sends.append((item, pos, there_pos, direction))
        cp = copy_of(item, pos, "core", slab(item, pos, c), sibling)
        cp.start()
        sends.append((item, pos, pos, "core"))

    def receive(item, pos):
        copy_of(item, pos, "link", slab(item, pos, c), sibling).wait_recv()
        pass_on(item, pos)

    def receive_core(item, pos):
        copy_of(item, pos, "core", slab(item, pos, 1 - c), sibling).wait_recv()

    swap_x = pltpu.make_async_remote_copy(
        src_ref=x_ref.at[0], dst_ref=xs, send_sem=swap_ssem, recv_sem=swap_rsem, device_id=across, device_id_type=MESH
    )
    for entry in EARLY:
        if entry == "swap":
            @pl.when(swapped)
            def _():
                swap_x.start()
        elif entry == "rest":
            load_out.wait()
            for first in range(0, width, 512):
                wo[h, first:first + 512, :] = stage[0:slab_out, first:first + 512].T
        elif entry[1] == "own":
            pass_on(*entry)
        else:
            receive(*entry)
    for item in (0, 1):
        for pos in POSITIONS:
            receive_core(item, pos)

    @pl.when(swapped)
    def _():
        swap_x.wait_recv()

    @pl.when(jnp.logical_not(swapped))
    def _():
        load_x.wait()

    @pl.when(s == SECTIONS - 1)
    def _():
        load_g.wait()

    load_pm.wait()
    load_ph.wait()

    in_a[...] = nn(xs[...], pm_ref[...])
    in_b[...] = jnp.zeros_like(in_b)
    steps = hidden_width // tile

    @pl.loop(0, steps)
    def _(i):
        for at, (item, pos) in enumerate(LATE[:-LAST]):
            @pl.when(i == at * steps // len(LATE[:-LAST]))
            def _():
                receive(item, pos)

        cols = pl.ds(pl.multiple_of(i * tile, tile), tile)
        for part in range(tokens // 256):
            rows = pl.ds(part * 256, 256)
            u = nt(xs[rows, 0:tile], wi[0, cols, :])
            for chip in range(1, CHIPS):
                u = u + nt(xs[rows, chip * tile:(chip + 1) * tile], wi[chip, cols, :])
            act, slant = gelu_parts(u)
            slope[rows, cols] = slant
            in_b[rows, :] += nn(act.astype(jnp.bfloat16), ph_ref[cols, :])

    for item, pos in LATE[-LAST:]:
        receive(item, pos)
    for item in (2, 3):
        for pos in POSITIONS:
            receive_core(item, pos)

    def chunk_copy(p, d, src, dst, send, recv, there):
        where = (pl.ds(pl.multiple_of(p * piece, piece), piece), pl.ds(d * chunk, chunk))
        return pltpu.make_async_remote_copy(
            src_ref=src.at[where], dst_ref=dst.at[where], send_sem=send.at[p, d], recv_sem=recv.at[p, d],
            device_id=there, device_id_type=MESH,
        )

    def to_next(p, d):
        return chunk_copy(p, d, stage, inbox, next_ssem, next_rsem, below)

    def to_skip(p, d):
        return chunk_copy(p, d, stage, skipbox, skip_ssem, skip_rsem, mirror)

    def outer(a, b):
        return lax.dot_general(
            a, b, (((0,), (0,)), ((), ())), precision=lax.Precision.HIGHEST,
            preferred_element_type=jnp.float32,
        )

    def last_copy(t, sample, index):
        return pltpu.make_async_remote_copy(
            src_ref=term.at[sample, pl.ds(t * 8, 8), :], dst_ref=parts.at[index, sample],
            send_sem=last_ssem.at[t, sample], recv_sem=last_rsem.at[index, sample],
            device_id=device(t, home_hi, x, c), device_id_type=MESH,
        )

    def finish(sample):
        rows = pl.ds(sample * SEQ, SEQ)
        out_a = nn(gu[rows, :], ph_ref[...])
        out_b = nn(inbox[rows, :], pm_ref[...])
        first = outer(in_a[rows, :], out_a)
        second = pltpu.roll(outer(in_b[rows, :], out_b), 64, 1)
        term[sample] = (first[0:64, :] + second[64:128, :]) * (SEQ ** -0.5)
        for t in range(SECTIONS):
            stays = (s == t) & jnp.logical_not(swapped)

            @pl.when(stays)
            def _():
                parts[t, sample] = term[sample, t * 8:(t + 1) * 8, :]

            @pl.when(jnp.logical_not(stays))
            def _():
                last_copy(t, sample, s).start()

    half = SECTIONS // 2
    gain_row = jnp.clip(half - 1 - s, 0, half - 1)

    @pl.loop(0, PIECES)
    def _(p):
        rows = pl.ds(pl.multiple_of(p * piece, piece), piece)
        for part in range(PARTS):
            cols = pl.ds(part * (width // PARTS), width // PARTS)
            chunks = range(part * CHUNKS // PARTS, (part + 1) * CHUNKS // PARTS)

            @pl.when(s < SECTIONS - 1)
            def _():
                for d in chunks:
                    to_next(p, d).wait_recv()

            @pl.when(s < half - 1)
            def _():
                for d in chunks:
                    to_skip(p, d).wait_recv()
                gain = gain_ref[pl.ds(gain_row, 1), cols]
                total = inbox[rows, cols].astype(jnp.float32) + gain * skipbox[rows, cols].astype(jnp.float32)
                inbox[rows, cols] = total.astype(jnp.bfloat16)

            @pl.when(s == half - 1)
            def _():
                gain = gain_ref[pl.ds(gain_row, 1), cols]
                value = inbox[rows, cols].astype(jnp.float32)
                inbox[rows, cols] = (value + gain * value).astype(jnp.bfloat16)

            @pl.loop(0, hidden_width // (4 * tile))
            def _(group):
                for one in range(4):
                    j = group * 4 + one
                    there = pl.ds(pl.multiple_of(j * tile, tile), tile)
                    product = nn(inbox[rows, cols], wo[j, cols, :])
                    if part == 0:
                        acc[:, there] = product
                    elif part < PARTS - 1:
                        acc[:, there] += product
                    else:
                        gu[rows, there] = ((acc[:, there] + product) * slope[rows, there]).astype(jnp.bfloat16)

        first_turn = (s == SECTIONS - 1) & (p == 0)

        @pl.when(first_turn & (c == 1))
        def _():
            pl.semaphore_wait(turn_sem, 1)

        @pl.when(s > 0)
        def _():
            for d in range(CHUNKS):
                @pl.loop(0, chunk // tile)
                def _(k):
                    there = pl.ds(pl.multiple_of(d * chunk + k * tile, tile), tile)
                    grad_x = nn(gu[rows, :], wi[d * (chunk // tile) + k])
                    stage[rows, there] = (inbox[rows, there].astype(jnp.float32) + grad_x).astype(jnp.bfloat16)

                to_next(p, d).start()

        for q in range(PIECES):
            soon = (s == half + 1) & (p == min(q + 1, PIECES - 1))
            @pl.when(soon | ((s > half + 1) & (p == PIECES - 1)))
            def _():
                for d in range(CHUNKS):
                    to_skip(q, d).start()

        for sample in range(samples - 1):
            @pl.when((s == 0) & (p == (sample + 1) * SEQ // piece - 1))
            def _():
                finish(sample)

        @pl.when(first_turn & (c == 0))
        def _():
            pl.semaphore_signal(turn_sem, inc=1, device_id=sibling, device_id_type=MESH)

    @pl.when(s > 0)
    def _():
        for sample in range(samples - 1):
            finish(sample)

    finish(samples - 1)

    for item, pos, there_pos, direction in sends:
        if direction == "core":
            copy_of(item, pos, "core", slab(item, pos, c), sibling).wait_send()
        else:
            copy_of(item, there_pos, "link", source(item, pos, there_pos), toward[direction]).wait_send()

    @pl.when(swapped)
    def _():
        swap_x.wait_send()

    @pl.loop(0, PIECES)
    def _(p):
        for d in range(CHUNKS):
            @pl.when(s > 0)
            def _():
                to_next(p, d).wait_send()

            @pl.when(s > half)
            def _():
                to_skip(p, d).wait_send()

    for t in range(SECTIONS):
        stays = (s == t) & jnp.logical_not(swapped)

        @pl.when(jnp.logical_not(stays))
        def _():
            for sample in range(samples):
                last_copy(t, sample, s).wait_send()
                last_copy(t, sample, t).wait_recv()

    total = parts[0]
    for t in range(1, SECTIONS):
        total = total + parts[t]
    out_ref[...] = total


def body(saved_inputs, grad_out, w_in, w_out, skip_gain, proj_model, proj_hidden):
    tokens, width = grad_out.shape
    hidden_width = w_in.shape[2]
    samples = tokens // SEQ
    bf16, f32 = jnp.bfloat16, jnp.float32
    dma = pltpu.SemaphoreType.DMA
    result = pl.pallas_call(
        kernel,
        out_shape=jax.ShapeDtypeStruct((samples, 8, 128), f32),
        in_specs=[pl.BlockSpec(memory_space=pl.ANY)] * 4 + [pl.BlockSpec(memory_space=pltpu.VMEM)] + [pl.BlockSpec(memory_space=pl.ANY)] * 2,
        out_specs=pl.BlockSpec(memory_space=pltpu.VMEM),
        scratch_shapes=[
            pltpu.VMEM((CHIPS, hidden_width, 256), bf16),
            pltpu.VMEM((2 * CHIPS, width, 256), bf16),
            pltpu.VMEM((tokens, width), bf16),
            pltpu.VMEM((tokens, hidden_width), f32),
            pltpu.VMEM((tokens, width), bf16),
            pltpu.VMEM((tokens, width), bf16),
            pltpu.VMEM((tokens, width), bf16),
            pltpu.VMEM((tokens, hidden_width), bf16),
            pltpu.VMEM((tokens // PIECES, hidden_width), f32),
            pltpu.VMEM((tokens, 128), f32),
            pltpu.VMEM((tokens, 128), f32),
            pltpu.VMEM((samples, 64, 128), f32),
            pltpu.VMEM((SECTIONS, samples, 8, 128), f32),
            dma((6,)),
            dma((len(EVENTS),)),
            dma((len(EVENTS),)),
            dma,
            dma,
            dma((PIECES, CHUNKS)),
            dma((PIECES, CHUNKS)),
            dma((PIECES, CHUNKS)),
            dma((PIECES, CHUNKS)),
            dma((SECTIONS, samples)),
            dma((SECTIONS, samples)),
            pltpu.SemaphoreType.REGULAR,
            pltpu.VMEM(proj_model.shape[1:], bf16),
            pltpu.VMEM(proj_hidden.shape[1:], bf16),
        ],
        compiler_params=pltpu.CompilerParams(
            collective_id=0, has_side_effects=True, vmem_limit_bytes=62 * 2**20
        ),
    )(saved_inputs, grad_out, w_in, w_out, skip_gain, proj_model, proj_hidden)
    return result[:, :, :64].reshape(samples, 512)


def solution(mesh):
    placed = (
        P("section", "shard", None),
        P("shard", None),
        P("section", "shard", None),
        P("section", "shard", None),
        P(),
        P("section", None, None),
        P("section", None, None),
    )
    return jax.shard_map(
        body, mesh=mesh, in_specs=placed, out_specs=P("shard", "section"), check_vma=False
    )
```

```python
import functools
import math

import jax
import jax.numpy as jnp
from jax import lax
from jax.experimental import pallas as pl
from jax.experimental.pallas import tpu as pltpu
from jax.sharding import PartitionSpec as P

MESH = pl.DeviceIdType.MESH
SEQ = 256
SECTIONS = 8
CHIPS = 8
PIECES = 4
CHUNKS = 4
PARTS = 2
square_root_half = 1.0 / math.sqrt(2.0)
inv_root_two_pi = 1.0 / math.sqrt(2.0 * math.pi)

POSITIONS = ("own", "xm", "xp", "x2a", "x2b", "yo", "pm", "pp", "p2a", "p2b")
ITEMS = (
    ("in", 0, 1920, False),
    ("in", 1920, 2176, True),
    ("out", 0, 960, False),
    ("out", 960, 1088, True),
)
EVENTS = {}
for _item in range(len(ITEMS)):
    for _pos in POSITIONS:
        if _pos != "own":
            EVENTS[(_item, _pos, "link")] = len(EVENTS)
        EVENTS[(_item, _pos, "core")] = len(EVENTS)


EARLY = (
    (0, "own"), (1, "own"), "rest",
    (0, "xm"), (0, "xp"), (1, "yo"), (1, "xm"), (1, "xp"), (0, "yo"), (0, "x2a"), (0, "x2b"),
    (2, "own"), (3, "own"), "swap",
    (1, "pm"), (1, "pp"), (0, "pm"), (0, "pp"), (1, "x2a"), (1, "x2b"), (2, "xm"), (2, "xp"),
    (0, "p2a"), (0, "p2b"), (1, "p2a"), (1, "p2b"),
)
LATE = (
    (3, "yo"), (3, "xm"), (3, "xp"), (2, "yo"), (2, "x2a"), (2, "x2b"), (3, "pm"), (3, "pp"),
    (2, "pm"), (2, "pp"), (3, "x2a"), (3, "x2b"), (2, "p2a"), (2, "p2b"), (3, "p2a"), (3, "p2b"),
)
LAST = 4


def forwards(pos, y_first):
    table = {
        "own": [("xm", "right"), ("xp", "left"), ("yo", "across")],
        "xm": [("x2a", "right")],
        "xp": [("x2b", "left")],
        "x2a": [],
        "x2b": [],
        "yo": [],
        "pm": [],
        "pp": [],
        "p2a": [],
        "p2b": [],
    }
    if y_first:
        table["yo"] = [("pm", "right"), ("pp", "left")]
        table["pm"] = [("p2a", "right")]
        table["pp"] = [("p2b", "left")]
    else:
        table["xm"] = table["xm"] + [("pm", "across")]
        table["xp"] = table["xp"] + [("pp", "across")]
        table["x2a"] = [("p2a", "across")]
        table["x2b"] = [("p2b", "across")]
    return table[pos]


def gelu_parts(value):
    cumulative = 0.5 * (1.0 + lax.erf(value * square_root_half))
    density = jnp.exp(-0.5 * value * value) * inv_root_two_pi
    return (value * cumulative, cumulative + value * density)


def nt(a, b):
    return lax.dot_general(a, b, (((1,), (1,)), ((), ())), preferred_element_type=jnp.float32)


def nn(a, b):
    return jnp.dot(a, b, preferred_element_type=jnp.float32)


def kernel(
    x_ref, g_ref, wi_ref, wo_ref, gain_ref, pm_hbm, ph_hbm, out_ref,
    wi, wo, xs, slope, inbox, skipbox, stage, gu, acc, in_a, in_b, term, parts,
    load_sem, ssem, rsem, swap_ssem, swap_rsem,
    next_ssem, next_rsem, skip_ssem, skip_rsem, last_ssem, last_rsem, turn_sem, pm_ref, ph_ref,
):
    s = lax.axis_index("section")
    h = lax.axis_index("shard")
    yh, x, c = h // 8, (h // 2) % 4, h % 2

    def crosses(section):
        return (lax.rem(section, 2) == 0) & (section < SECTIONS - 2)

    tokens, width = xs.shape
    hidden_width = slope.shape[1]
    piece = tokens // PIECES
    samples = tokens // SEQ
    chunk = width // CHUNKS
    tile = 256

    def device(section, hi, xx, core):
        return (section, hi * 8 + xx * 2 + core)

    right = device(s, yh, (x + 1) % 4, c)
    left = device(s, yh, (x + 3) % 4, c)
    across = device(s, 1 - yh, x, c)
    sibling = device(s, yh, x, 1 - c)
    swapped = crosses(s) & (c == 1)

    def facing(section):
        cross = (crosses(s) | crosses(section)) & (c == 1)
        return device(section, jnp.where(cross, 1 - yh, yh), x, c)

    below = facing(jnp.maximum(s - 1, 0))
    mirror = facing(SECTIONS - 1 - s)
    home_hi = jnp.where(swapped, 1 - yh, yh)
    toward = {"right": right, "left": left, "across": across}

    barrier = pltpu.get_barrier_semaphore()
    for there in (right, left, sibling, across):
        pl.semaphore_signal(barrier, inc=1, device_id=there, device_id_type=MESH)
    for step in range(1, SECTIONS):
        for hi in range(2):
            pl.semaphore_signal(
                barrier, inc=1, device_id=device((s + step) % SECTIONS, hi, x, c), device_id_type=MESH
            )

    own_chip = yh * 4 + x
    slab_in, slab_out = wi_ref.shape[1], wo_ref.shape[1]
    load_in = pltpu.make_async_copy(wi_ref.at[0], gu.at[pl.ds(0, slab_in)], load_sem.at[0])
    load_out = pltpu.make_async_copy(wo_ref.at[0], stage.at[pl.ds(0, slab_out)], load_sem.at[1])
    load_x = pltpu.make_async_copy(x_ref.at[0], xs, load_sem.at[2])
    load_g = pltpu.make_async_copy(g_ref, inbox, load_sem.at[3])
    load_pm = pltpu.make_async_copy(pm_hbm.at[0], pm_ref, load_sem.at[4])
    load_ph = pltpu.make_async_copy(ph_hbm.at[0], ph_ref, load_sem.at[5])
    load_in.start()
    load_out.start()
    load_pm.start()
    load_ph.start()
    @pl.when(jnp.logical_not(swapped))
    def _():
        load_x.start()

    @pl.when(s == SECTIONS - 1)
    def _():
        load_g.start()

    load_in.wait()
    own_cols = pl.ds(pl.multiple_of(c * slab_in, slab_in), slab_in)
    for first in range(0, hidden_width, 512):
        wi[own_chip, first:first + 512, own_cols] = gu[0:slab_in, first:first + 512].T
    pl.semaphore_wait(barrier, 4 + 2 * (SECTIONS - 1))

    def slab(item, pos, core):
        array, first, rows, _ = ITEMS[item]
        hi = yh if pos in ("own", "xm", "xp", "x2a", "x2b") else 1 - yh
        step = {"own": 0, "yo": 0, "xm": 3, "pm": 3, "xp": 1, "pp": 1}.get(pos, 2)
        half = pos[-1] if pos[-1] in "ab" else ""
        return slab_at(array, hi * 4 + (x + step) % 4, core, first, rows, half)

    def slab_at(array, chip, core, first, rows, half):
        if half:
            rows = rows // 2
            first = first + (rows if half == "b" else 0)
        if array == "in":
            return wi.at[chip, pl.ds(first, rows), pl.ds(pl.multiple_of(core * 128, 128), 128)]
        return wo.at[chip * 2 + core, pl.ds(first, rows), :]

    def copy_of(item, pos, kind, src, there):
        event = EVENTS[(item, pos, kind)]
        return pltpu.make_async_remote_copy(
            src_ref=src, dst_ref=src, send_sem=ssem.at[event], recv_sem=rsem.at[event],
            device_id=there, device_id_type=MESH,
        )

    def source(item, pos, there_pos):
        array, first, rows, _ = ITEMS[item]
        half = there_pos[-1] if there_pos[-1] in "ab" else ""
        hi = yh if pos in ("own", "xm", "xp", "x2a", "x2b") else 1 - yh
        step = {"own": 0, "yo": 0, "xm": 3, "pm": 3, "xp": 1, "pp": 1}.get(pos, 2)
        return slab_at(array, hi * 4 + (x + step) % 4, c, first, rows, half)

    sends = []

    def pass_on(item, pos):
        for there_pos, direction in forwards(pos, ITEMS[item][3]):
            cp = copy_of(item, there_pos, "link", source(item, pos, there_pos), toward[direction])
            cp.start()
            sends.append((item, pos, there_pos, direction))
        cp = copy_of(item, pos, "core", slab(item, pos, c), sibling)
        cp.start()
        sends.append((item, pos, pos, "core"))

    def receive(item, pos):
        copy_of(item, pos, "link", slab(item, pos, c), sibling).wait_recv()
        pass_on(item, pos)

    def receive_core(item, pos):
        copy_of(item, pos, "core", slab(item, pos, 1 - c), sibling).wait_recv()

    swap_x = pltpu.make_async_remote_copy(
        src_ref=x_ref.at[0], dst_ref=xs, send_sem=swap_ssem, recv_sem=swap_rsem, device_id=across, device_id_type=MESH
    )
    for entry in EARLY:
        if entry == "swap":
            @pl.when(swapped)
            def _():
                swap_x.start()
        elif entry == "rest":
            load_out.wait()
            for first in range(0, width, 512):
                wo[h, first:first + 512, :] = stage[0:slab_out, first:first + 512].T
        elif entry[1] == "own":
            pass_on(*entry)
        else:
            receive(*entry)
    for item in (0, 1):
        for pos in POSITIONS:
            receive_core(item, pos)

    @pl.when(swapped)
    def _():
        swap_x.wait_recv()

    @pl.when(jnp.logical_not(swapped))
    def _():
        load_x.wait()

    @pl.when(s == SECTIONS - 1)
    def _():
        load_g.wait()

    load_pm.wait()
    load_ph.wait()

    in_a[...] = nn(xs[...], pm_ref[...])
    in_b[...] = jnp.zeros_like(in_b)
    steps = hidden_width // tile

    @pl.loop(0, steps)
    def _(i):
        for at, (item, pos) in enumerate(LATE[:-LAST]):
            @pl.when(i == at * steps // len(LATE[:-LAST]))
            def _():
                receive(item, pos)

        cols = pl.ds(pl.multiple_of(i * tile, tile), tile)
        for part in range(tokens // 256):
            rows = pl.ds(part * 256, 256)
            u = nt(xs[rows, 0:tile], wi[0, cols, :])
            for chip in range(1, CHIPS):
                u = u + nt(xs[rows, chip * tile:(chip + 1) * tile], wi[chip, cols, :])
            act, slant = gelu_parts(u)
            slope[rows, cols] = slant
            in_b[rows, :] += nn(act.astype(jnp.bfloat16), ph_ref[cols, :])

    for item, pos in LATE[-LAST:]:
        receive(item, pos)
    for item in (2, 3):
        for pos in POSITIONS:
            receive_core(item, pos)

    def chunk_copy(p, d, src, dst, send, recv, there):
        where = (pl.ds(pl.multiple_of(p * piece, piece), piece), pl.ds(d * chunk, chunk))
        return pltpu.make_async_remote_copy(
            src_ref=src.at[where], dst_ref=dst.at[where], send_sem=send.at[p, d], recv_sem=recv.at[p, d],
            device_id=there, device_id_type=MESH,
        )

    def to_next(p, d):
        return chunk_copy(p, d, stage, inbox, next_ssem, next_rsem, below)

    def to_skip(p, d):
        return chunk_copy(p, d, stage, skipbox, skip_ssem, skip_rsem, mirror)

    def outer(a, b):
        return lax.dot_general(
            a, b, (((0,), (0,)), ((), ())), precision=lax.Precision.HIGHEST,
            preferred_element_type=jnp.float32,
        )

    def last_copy(t, sample, index):
        return pltpu.make_async_remote_copy(
            src_ref=term.at[sample, pl.ds(t * 8, 8), :], dst_ref=parts.at[index, sample],
            send_sem=last_ssem.at[t, sample], recv_sem=last_rsem.at[index, sample],
            device_id=device(t, home_hi, x, c), device_id_type=MESH,
        )

    def finish(sample):
        rows = pl.ds(sample * SEQ, SEQ)
        out_a = nn(gu[rows, :], ph_ref[...])
        out_b = nn(inbox[rows, :], pm_ref[...])
        first = outer(in_a[rows, :], out_a)
        second = pltpu.roll(outer(in_b[rows, :], out_b), 64, 1)
        term[sample] = (first[0:64, :] + second[64:128, :]) * (SEQ ** -0.5)
        for t in range(SECTIONS):
            stays = (s == t) & jnp.logical_not(swapped)

            @pl.when(stays)
            def _():
                parts[t, sample] = term[sample, t * 8:(t + 1) * 8, :]

            @pl.when(jnp.logical_not(stays))
            def _():
                last_copy(t, sample, s).start()

    half = SECTIONS // 2
    gain_row = jnp.clip(half - 1 - s, 0, half - 1)

    def gather_sent():
        for item, pos, there_pos, direction in sends:
            if direction == "core":
                copy_of(item, pos, "core", slab(item, pos, c), sibling).wait_send()
            else:
                copy_of(item, there_pos, "link", source(item, pos, there_pos), toward[direction]).wait_send()

    @pl.when(s < half)
    def _():
        gather_sent()

    @pl.loop(0, PIECES)
    def _(p):
        rows = pl.ds(pl.multiple_of(p * piece, piece), piece)
        for part in range(PARTS):
            cols = pl.ds(part * (width // PARTS), width // PARTS)
            chunks = range(part * CHUNKS // PARTS, (part + 1) * CHUNKS // PARTS)

            @pl.when(s < SECTIONS - 1)
            def _():
                for d in chunks:
                    to_next(p, d).wait_recv()

            @pl.when(s < half - 1)
            def _():
                for d in chunks:
                    to_skip(p, d).wait_recv()
                gain = gain_ref[pl.ds(gain_row, 1), cols]
                total = inbox[rows, cols].astype(jnp.float32) + gain * skipbox[rows, cols].astype(jnp.float32)
                inbox[rows, cols] = total.astype(jnp.bfloat16)

            @pl.when(s == half - 1)
            def _():
                gain = gain_ref[pl.ds(gain_row, 1), cols]
                value = inbox[rows, cols].astype(jnp.float32)
                inbox[rows, cols] = (value + gain * value).astype(jnp.bfloat16)

            @pl.loop(0, hidden_width // (8 * tile))
            def _(group):
                for one in range(8):
                    j = group * 8 + one
                    there = pl.ds(pl.multiple_of(j * tile, tile), tile)
                    product = nn(inbox[rows, cols], wo[j, cols, :])
                    if part == 0:
                        acc[:, there] = product
                    elif part < PARTS - 1:
                        acc[:, there] += product
                    else:
                        gu[rows, there] = ((acc[:, there] + product) * slope[rows, there]).astype(jnp.bfloat16)

        first_turn = (s == SECTIONS - 1) & (p == 0)

        @pl.when(first_turn & (c == 1))
        def _():
            pl.semaphore_wait(turn_sem, 1)

        @pl.when(s > 0)
        def _():
            for d in range(CHUNKS):
                @pl.loop(0, chunk // tile)
                def _(k):
                    there = pl.ds(pl.multiple_of(d * chunk + k * tile, tile), tile)
                    grad_x = nn(gu[rows, :], wi[d * (chunk // tile) + k])
                    stage[rows, there] = (inbox[rows, there].astype(jnp.float32) + grad_x).astype(jnp.bfloat16)

                to_next(p, d).start()

        for q in range(PIECES):
            soon = (s == half + 1) & (p == min(q + 1, PIECES - 1))
            @pl.when(soon | ((s > half + 1) & (p == PIECES - 1)))
            def _():
                for d in range(CHUNKS):
                    to_skip(q, d).start()

        for sample in range(samples - 1):
            @pl.when((s == 0) & (p == (sample + 1) * SEQ // piece - 1))
            def _():
                finish(sample)

        @pl.when(first_turn & (c == 0))
        def _():
            pl.semaphore_signal(turn_sem, inc=1, device_id=sibling, device_id_type=MESH)

    @pl.when(s > 0)
    def _():
        for sample in range(samples - 1):
            finish(sample)

    finish(samples - 1)

    @pl.when(s >= half)
    def _():
        gather_sent()

    @pl.when(swapped)
    def _():
        swap_x.wait_send()

    @pl.loop(0, PIECES)
    def _(p):
        for d in range(CHUNKS):
            @pl.when(s > 0)
            def _():
                to_next(p, d).wait_send()

            @pl.when(s > half)
            def _():
                to_skip(p, d).wait_send()

    for t in range(SECTIONS):
        stays = (s == t) & jnp.logical_not(swapped)

        @pl.when(jnp.logical_not(stays))
        def _():
            for sample in range(samples):
                last_copy(t, sample, s).wait_send()
                last_copy(t, sample, t).wait_recv()

    total = parts[0]
    for t in range(1, SECTIONS):
        total = total + parts[t]
    out_ref[...] = total


def body(saved_inputs, grad_out, w_in, w_out, skip_gain, proj_model, proj_hidden):
    tokens, width = grad_out.shape
    hidden_width = w_in.shape[2]
    samples = tokens // SEQ
    bf16, f32 = jnp.bfloat16, jnp.float32
    dma = pltpu.SemaphoreType.DMA
    result = pl.pallas_call(
        kernel,
        out_shape=jax.ShapeDtypeStruct((samples, 8, 128), f32),
        in_specs=[pl.BlockSpec(memory_space=pl.ANY)] * 4 + [pl.BlockSpec(memory_space=pltpu.VMEM)] + [pl.BlockSpec(memory_space=pl.ANY)] * 2,
        out_specs=pl.BlockSpec(memory_space=pltpu.VMEM),
        scratch_shapes=[
            pltpu.VMEM((CHIPS, hidden_width, 256), bf16),
            pltpu.VMEM((2 * CHIPS, width, 256), bf16),
            pltpu.VMEM((tokens, width), bf16),
            pltpu.VMEM((tokens, hidden_width), f32),
            pltpu.VMEM((tokens, width), bf16),
            pltpu.VMEM((tokens, width), bf16),
            pltpu.VMEM((tokens, width), bf16),
            pltpu.VMEM((tokens, hidden_width), bf16),
            pltpu.VMEM((tokens // PIECES, hidden_width), f32),
            pltpu.VMEM((tokens, 128), f32),
            pltpu.VMEM((tokens, 128), f32),
            pltpu.VMEM((samples, 64, 128), f32),
            pltpu.VMEM((SECTIONS, samples, 8, 128), f32),
            dma((6,)),
            dma((len(EVENTS),)),
            dma((len(EVENTS),)),
            dma,
            dma,
            dma((PIECES, CHUNKS)),
            dma((PIECES, CHUNKS)),
            dma((PIECES, CHUNKS)),
            dma((PIECES, CHUNKS)),
            dma((SECTIONS, samples)),
            dma((SECTIONS, samples)),
            pltpu.SemaphoreType.REGULAR,
            pltpu.VMEM(proj_model.shape[1:], bf16),
            pltpu.VMEM(proj_hidden.shape[1:], bf16),
        ],
        compiler_params=pltpu.CompilerParams(
            collective_id=0, has_side_effects=True, vmem_limit_bytes=62 * 2**20
        ),
    )(saved_inputs, grad_out, w_in, w_out, skip_gain, proj_model, proj_hidden)
    return result[:, :, :64].reshape(samples, 512)


def solution(mesh):
    placed = (
        P("section", "shard", None),
        P("shard", None),
        P("section", "shard", None),
        P("section", "shard", None),
        P(),
        P("section", None, None),
        P("section", None, None),
    )
    return jax.shard_map(
        body, mesh=mesh, in_specs=placed, out_specs=P("shard", "section"), check_vma=False
    )
```
